256 devices in a mesh: pair: 64 (over y_hi, z, x), row: 4 (over y_lo, core).
Axes of the slice: x: 4, y: 4 (y_hi: 2, y_lo: 2; y = y_hi * 2 + y_lo), z: 8, core: 2. Of those that a mesh axis runs over, the one named last changes fastest.
Arguments:
- states: float32 [8192, 32768], P('row', 'pair'), may hold values from -40 to 40, as said below
Outputs:
- rotated: float32 [8192, 32768], P('row', 'pair')
The draws below stay inside these ranges and needn't reach their ends.
Inputs may be any that keep to these rules, and one draw needn't show every extreme that they name: Real-valued states of full rank.
All inputs are finite; a program needn't handle non-finite values.
Results may differ from the reference program's by a relative error of at most 0.0001.
Values sent between devices are 32-bit elements; how exact they have to be, the bound alone decides.
A program may use at most 64 MiB of HBM per device.

```python
import jax
import jax.numpy as jnp
from jax import lax

BLK = 256
ROUNDS = 2
NS_STEPS = 2
SAMPLES = 8192
NCOL = 32768
N_PAIR = 64


def draw_states(key, part):
    key = jax.random.fold_in(key, 11)
    key_base, key_rows, key_cols = jax.random.split(key, 3)
    rows = jnp.exp(jax.random.uniform(key_rows, (SAMPLES, 1), jnp.float32, jnp.log(0.5), jnp.log(2.0)))
    cols = jnp.exp(jax.random.uniform(key_cols, (1, NCOL), jnp.float32, jnp.log(0.32), jnp.log(3.2)))
    base = jnp.clip(jax.random.normal(key_base, (SAMPLES, NCOL), jnp.float32), -4.0, 4.0)
    return (base * rows * cols).astype(jnp.float32)


def setup_inputs(seed: int = 0) -> dict:
    arg_keys = jax.random.split(jax.random.key(seed), 2)
    return {
        "states": draw_states(jax.random.fold_in(arg_keys[1], 71), 0),
    }


highest = lax.Precision.HIGHEST

def rotation(gram, width):
    diag = jnp.diagonal(gram)
    first = diag[:width]
    second = diag[width:]
    cross = gram[:width, width:]
    gap = second[None, :] - first[:, None]
    raw = cross * gap / (gap * gap + first[:, None] * second[None, :] + 1e-06)
    theta = raw / (1.0 + jnp.sqrt(jnp.sum(raw * raw)))
    ident = jnp.eye(width, dtype=gram.dtype)
    upper = jnp.concatenate([ident, theta], axis=1)
    lower = jnp.concatenate([-theta.T, ident], axis=1)
    mat = jnp.concatenate([upper, lower], axis=0)
    for step in range(NS_STEPS):
        square = jnp.dot(mat.T, mat, precision=highest, preferred_element_type=jnp.float32)
        mat = 1.5 * mat - 0.5 * jnp.dot(mat, square, precision=highest, preferred_element_type=jnp.float32)
    return mat

def rotate_pair(pair):
    gram = jnp.dot(pair.T, pair, precision=highest, preferred_element_type=jnp.float32)
    turn = rotation(gram, BLK)
    return jnp.dot(pair, turn, precision=highest, preferred_element_type=jnp.float32)

def reference(states):
    blocks = states.reshape(SAMPLES, N_PAIR, 2, BLK)
    top = jnp.transpose(blocks[:, :, 0, :], (1, 0, 2))
    bottom = jnp.transpose(blocks[:, :, 1, :], (1, 0, 2))
    for step in range(ROUNDS):
        pairs = jnp.concatenate([top, bottom], axis=2)
        turned = lax.map(rotate_pair, pairs)
        top = turned[:, :, :BLK]
        bottom = turned[:, :, BLK:]
        if step + 1 < ROUNDS:
            new_top = jnp.concatenate([top[:1], bottom[:1], top[1:-1]], axis=0)
            new_bottom = jnp.concatenate([bottom[1:], top[-1:]], axis=0)
            top = new_top
            bottom = new_bottom
    joined = jnp.stack([top, bottom], axis=2)
    return jnp.transpose(joined, (1, 0, 2, 3)).reshape(SAMPLES, NCOL)
```

```python
import functools

import jax
import jax.numpy as jnp
from jax import lax
from jax.experimental import pallas as pl
from jax.experimental.pallas import tpu as pltpu
from jax.sharding import PartitionSpec as P

MESH = pl.DeviceIdType.MESH
F32 = jnp.float32
BF16 = jnp.bfloat16
EXTRA = 8
PIECES = 2


def split(value):
    high = value.astype(BF16)
    return high, (value - high.astype(F32)).astype(BF16)


def dot(left, right, dims):
    return lax.dot_general(left, right, (dims, ((), ())), preferred_element_type=F32)


def dot3(left, right, dims=((1,), (0,))):
    lh, ll = left
    rh, rl = right
    return dot(lh, rh, dims) + (dot(lh, rl, dims) + dot(ll, rh, dims))


def inner(left, right):
    return dot3(left, right, ((0,), (0,)))


def column_sums(value):
    rows, width = value.shape
    return jnp.sum((value * value).reshape(rows // EXTRA, EXTRA, width), axis=0)


def angles(cross, first, second):
    width = cross.shape[0]
    first = jnp.broadcast_to(first, (width, width)).T
    second = jnp.broadcast_to(second, (width, width))
    gap = second - first
    raw = cross * gap / (gap * gap + first * second + 1e-06)
    total = jnp.sum(jnp.sum(raw * raw, axis=0, keepdims=True), axis=1, keepdims=True)
    return raw / (1.0 + jnp.sqrt(total))


def polynomial(square, ident):
    halves = split(square)
    second = dot3(halves, halves)
    factor = 0.375 * ident - 0.3125 * square + 0.0625 * second
    return ident - 0.5 * square + dot3(split(second), split(factor))


def write_turn(theta, high_ref, low_ref):
    width = theta.shape[0]
    rows = lax.broadcasted_iota(jnp.int32, (width, width), 0)
    cols = lax.broadcasted_iota(jnp.int32, (width, width), 1)
    ident = jnp.where(rows == cols, 1.0, 0.0).astype(F32)
    plain = split(theta)
    flipped = split(theta.T)
    upper = polynomial(dot3(plain, flipped), ident)
    lower = polynomial(dot3(flipped, plain), ident)
    off = dot3(split(upper), plain)
    one, two = pl.ds(0, width), pl.ds(width, width)
    for at, block in (((one, one), upper), ((one, two), off), ((two, one), -off.T), ((two, two), lower)):
        high, low = split(block)
        high_ref[at] = high
        low_ref[at] = low


def exchange_kernel(
    n_pair, chunk, load,
    x_ref, pair_ref, high_ref, low_ref,
    top, bot, new_top, new_bot, part, got, full, acc, sums, turn_high, turn_low,
    load_sem, send_sem, recv_sem, store_sem, row_send, row_recv,
):
    p = lax.axis_index("pair")
    row = lax.axis_index("row")
    core = lax.rem(row, 2)
    mate = row + 1 - 2 * core
    across = lax.rem(row + 2, 4)
    samples, width = top.shape
    n_chunks = samples // chunk
    first = p == 0
    last = p == n_pair - 1

    loads = []
    for i in range(samples // load):
        at = pl.ds(i * load, load)
        for half, ref in enumerate((top, bot)):
            copy = pltpu.make_async_copy(
                x_ref.at[at, pl.ds(half * width, width)], ref.at[at], load_sem.at[half, i]
            )
            copy.start()
            loads.append(copy)

    barrier = pltpu.get_barrier_semaphore()

    def greet(**where):
        pl.semaphore_signal(barrier, inc=1, device_id=where, device_id_type=MESH)

    greet(row=mate)
    greet(row=across)

    @pl.when(jnp.logical_not(first))
    def _():
        greet(pair=p - 1)

    @pl.when(jnp.logical_not(last))
    def _():
        greet(pair=p + 1)

    def add_gram(tops, bots, fresh):
        cross = inner(split(tops), split(bots))
        one, two = column_sums(tops), column_sums(bots)
        if fresh:
            acc[...] = cross
            sums[0] = one
            sums[1] = two
        else:
            acc[...] += cross
            sums[0] += one
            sums[1] += two

    def row_sum(turn):
        size = width // 2
        step = size // PIECES

        def piece(k):
            return pl.ds(k * step, step + (EXTRA if k == PIECES - 1 else 0))

        def send(src, dst, stage, k, **where):
            return pltpu.make_async_remote_copy(
                src_ref=src, dst_ref=dst,
                send_sem=row_send.at[turn, stage, k], recv_sem=row_recv.at[turn, stage, k],
                device_id=where, device_id_type=MESH,
            )

        one = lambda k: send(part.at[turn, 1 - core, piece(k)], got.at[turn, 0, piece(k)], 0, k, row=mate)
        two = lambda k: send(part.at[turn, core, piece(k)], got.at[turn, 1, piece(k)], 1, k, row=across)
        three = lambda k: send(full.at[turn, core, piece(k)], full.at[turn, core, piece(k)], 2, k, row=mate)

        for h in range(2):
            part[turn, h, pl.ds(0, size)] = acc[pl.ds(h * size, size)]
            part[turn, h, pl.ds(size, EXTRA)] = sums[h]
        for k in range(PIECES):
            one(k).start()
        for k in range(PIECES):
            one(k).wait()
            part[turn, core, piece(k)] += got[turn, 0, piece(k)]
            two(k).start()
        for k in range(PIECES):
            two(k).wait()
            full[turn, core, piece(k)] = part[turn, core, piece(k)] + got[turn, 1, piece(k)]
            three(k).start()
        for k in range(PIECES):
            three(k).wait()
        cross = jnp.concatenate([full[turn, 0, pl.ds(0, size)], full[turn, 1, pl.ds(0, size)]], axis=0)
        diag = [jnp.sum(full[turn, h, pl.ds(size, EXTRA)], axis=0, keepdims=True) for h in range(2)]
        return angles(cross, *diag)

    for i in range(samples // load):
        loads[2 * i].wait()
        loads[2 * i + 1].wait()
        at = pl.ds(i * load, load)
        add_gram(top[at], bot[at], i == 0)

    @pl.when(jnp.logical_or(first, last))
    def _():
        pl.semaphore_wait(barrier, 3)

    @pl.when(jnp.logical_not(jnp.logical_or(first, last)))
    def _():
        pl.semaphore_wait(barrier, 4)

    write_turn(row_sum(0), turn_high, turn_low)

    def rows_of(i):
        return pl.ds(pl.multiple_of(i * chunk, chunk), chunk)

    def to(src, dst, side, i, **where):
        return pltpu.make_async_remote_copy(
            src_ref=src.at[rows_of(i)], dst_ref=dst.at[rows_of(i)],
            send_sem=send_sem.at[side, i], recv_sem=recv_sem.at[side, i],
            device_id=where, device_id_type=MESH,
        )

    def stays(src, dst, side, i):
        return pltpu.make_async_copy(src.at[rows_of(i)], dst.at[rows_of(i)], recv_sem.at[side, i])

    def rotate(i, carry):
        at = rows_of(i)
        value = split(jnp.concatenate([top[at], bot[at]], axis=1))
        out = dot3(value, (turn_high[...], turn_low[...]))
        top[at] = out[:, :width]
        bot[at] = out[:, width:]

        @pl.when(first)
        def _():
            to(bot, new_top, 0, i, pair=p + 1).start()
            stays(top, new_top, 0, i).start()

        @pl.when(jnp.logical_not(jnp.logical_or(first, last)))
        def _():
            to(top, new_top, 0, i, pair=p + 1).start()

        @pl.when(jnp.logical_not(first))
        def _():
            to(bot, new_bot, 1, i, pair=p - 1).start()

        @pl.when(last)
        def _():
            stays(top, new_bot, 1, i).start()

        return carry

    lax.fori_loop(0, n_chunks, rotate, 0)

    acc[...] = jnp.zeros_like(acc)
    sums[...] = jnp.zeros_like(sums)

    def store(ref, half, i):
        return pltpu.make_async_copy(
            ref.at[rows_of(i)], pair_ref.at[rows_of(i), pl.ds(half * width, width)], store_sem.at[half, i]
        )

    def receive(i, carry):
        @pl.when(first)
        def _():
            stays(top, new_top, 0, i).wait()

        @pl.when(jnp.logical_not(first))
        def _():
            to(top, new_top, 0, i, pair=p - 1).wait_recv()

        @pl.when(last)
        def _():
            stays(top, new_bot, 1, i).wait()

        @pl.when(jnp.logical_not(last))
        def _():
            to(bot, new_bot, 1, i, pair=p + 1).wait_recv()

        store(new_top, 0, i).start()
        store(new_bot, 1, i).start()
        at = rows_of(i)
        add_gram(new_top[at], new_bot[at], False)
        return carry

    lax.fori_loop(0, n_chunks, receive, 0)
    write_turn(row_sum(1), high_ref, low_ref)

    def finish(i, carry):
        store(new_top, 0, i).wait()
        store(new_bot, 1, i).wait()

        @pl.when(jnp.logical_not(last))
        def _():
            to(top, new_top, 0, i, pair=p + 1).wait_send()

        @pl.when(jnp.logical_not(first))
        def _():
            to(bot, new_bot, 1, i, pair=p - 1).wait_send()

        return carry

    lax.fori_loop(0, n_chunks, finish, 0)


def rotate_kernel(x_ref, high_ref, low_ref, out_ref):
    out_ref[...] = dot3(split(x_ref[...]), (high_ref[...], low_ref[...]))


def shards(n_pair, states):
    samples, both = states.shape
    width = both // 2
    chunk = 128
    load = 256
    n_chunks = samples // chunk
    pair, high, low = pl.pallas_call(
        functools.partial(exchange_kernel, n_pair, chunk, load),
        out_shape=[
            jax.ShapeDtypeStruct((samples, both), F32),
            jax.ShapeDtypeStruct((both, both), BF16),
            jax.ShapeDtypeStruct((both, both), BF16),
        ],
        in_specs=[pl.BlockSpec(memory_space=pltpu.HBM)],
        out_specs=[
            pl.BlockSpec(memory_space=pl.ANY),
            pl.BlockSpec(memory_space=pltpu.VMEM),
            pl.BlockSpec(memory_space=pltpu.VMEM),
        ],
        scratch_shapes=[pltpu.VMEM((samples, width), F32)] * 4
        + [
            pltpu.VMEM((2, 2, width // 2 + EXTRA, width), F32),
            pltpu.VMEM((2, 2, width // 2 + EXTRA, width), F32),
            pltpu.VMEM((2, 2, width // 2 + EXTRA, width), F32),
            pltpu.VMEM((width, width), F32),
            pltpu.VMEM((2, EXTRA, width), F32),
            pltpu.VMEM((both, both), BF16),
            pltpu.VMEM((both, both), BF16),
            pltpu.SemaphoreType.DMA((2, samples // load)),
            pltpu.SemaphoreType.DMA((2, n_chunks)),
            pltpu.SemaphoreType.DMA((2, n_chunks)),
            pltpu.SemaphoreType.DMA((2, n_chunks)),
            pltpu.SemaphoreType.DMA((2, 3, PIECES)),
            pltpu.SemaphoreType.DMA((2, 3, PIECES)),
        ],
        compiler_params=pltpu.CompilerParams(
            collective_id=0, has_side_effects=True, vmem_limit_bytes=40 * 2**20
        ),
        name="exchange",
    )(states)
    tile = 256
    return pl.pallas_call(
        rotate_kernel,
        grid=(samples // tile,),
        out_shape=jax.ShapeDtypeStruct((samples, both), F32),
        in_specs=[
            pl.BlockSpec((tile, both), lambda i: (i, 0)),
            pl.BlockSpec((both, both), lambda i: (0, 0)),
            pl.BlockSpec((both, both), lambda i: (0, 0)),
        ],
        out_specs=pl.BlockSpec((tile, both), lambda i: (i, 0)),
        compiler_params=pltpu.CompilerParams(vmem_limit_bytes=20 * 2**20),
        name="rotate",
    )(pair, high, low)


def solution(mesh):
    spec = P("row", "pair")
    return jax.shard_map(
        functools.partial(shards, mesh.shape["pair"]),
        mesh=mesh, in_specs=(spec,), out_specs=spec, check_vma=False,
    )
```

```python
import functools

import jax
import jax.numpy as jnp
from jax import lax
from jax.experimental import pallas as pl
from jax.experimental.pallas import tpu as pltpu
from jax.sharding import PartitionSpec as P

MESH = pl.DeviceIdType.MESH
F32 = jnp.float32
BF16 = jnp.bfloat16
EXTRA = 8
PIECES = 2


def split(value):
    high = value.astype(BF16)
    return high, (value - high.astype(F32)).astype(BF16)


def dot(left, right, dims):
    return lax.dot_general(left, right, (dims, ((), ())), preferred_element_type=F32)


def dot3(left, right, dims=((1,), (0,))):
    lh, ll = left
    rh, rl = right
    return dot(lh, rh, dims) + (dot(lh, rl, dims) + dot(ll, rh, dims))


def inner(left, right):
    return dot3(left, right, ((0,), (0,)))


def column_sums(value):
    rows, width = value.shape
    return jnp.sum((value * value).reshape(rows // EXTRA, EXTRA, width), axis=0)


def angles(cross, first, second):
    width = cross.shape[0]
    first = jnp.broadcast_to(first, (width, width)).T
    second = jnp.broadcast_to(second, (width, width))
    gap = second - first
    raw = cross * gap / (gap * gap + first * second + 1e-06)
    total = jnp.sum(jnp.sum(raw * raw, axis=0, keepdims=True), axis=1, keepdims=True)
    return raw / (1.0 + jnp.sqrt(total))


def polynomial(square, ident):
    halves = split(square)
    second = dot3(halves, halves)
    factor = 0.375 * ident - 0.3125 * square + 0.0625 * second
    return ident - 0.5 * square + dot3(split(second), split(factor))


def write_turn(theta, high_ref, low_ref):
    width = theta.shape[0]
    rows = lax.broadcasted_iota(jnp.int32, (width, width), 0)
    cols = lax.broadcasted_iota(jnp.int32, (width, width), 1)
    ident = jnp.where(rows == cols, 1.0, 0.0).astype(F32)
    plain = split(theta)
    flipped = split(theta.T)
    upper = polynomial(dot3(plain, flipped), ident)
    lower = polynomial(dot3(flipped, plain), ident)
    off = dot3(split(upper), plain)
    one, two = pl.ds(0, width), pl.ds(width, width)
    for half, at, block in ((0, one, upper), (1, one, off), (0, two, -off.T), (1, two, lower)):
        high, low = split(block)
        high_ref[half, at] = high
        low_ref[half, at] = low


def exchange_kernel(
    n_pair, chunk, load, early,
    x_ref, pair_ref, high_ref, low_ref,
    x, out, raw, part, got, full, acc, sums, theta_own, thetas, turn_high, turn_low, early_high, early_low, relay,
    load_sem, send_sem, recv_sem, raw_send, raw_recv, theta_send, theta_recv, share_send, share_recv, row_send, row_recv,
    relay_send, relay_recv,
):
    p = lax.axis_index("pair")
    row = lax.axis_index("row")
    core = lax.rem(row, 2)
    mate = row + 1 - 2 * core
    across = lax.rem(row + 2, 4)
    others = (mate, across, 3 - row)
    samples, both = x.shape
    width = both // 2
    main = samples - early
    n_chunks = main // chunk
    first = p == 0
    last = p == n_pair - 1
    not_first = jnp.logical_not(first)
    not_last = jnp.logical_not(last)
    seam = n_pair // 2
    before = p == seam - 1
    after = p == seam
    ends = jnp.logical_or(first, last)
    middle = jnp.logical_or(before, after)
    rightward = jnp.logical_and(not_last, jnp.logical_not(before))
    leftward = jnp.logical_and(not_first, jnp.logical_not(after))
    inside = (jnp.logical_and(not_first, jnp.logical_not(after)), jnp.logical_and(not_last, jnp.logical_not(before)))
    halves = pl.ds(0, width), pl.ds(width, width)

    loads = []
    for i in range(samples // load):
        at = pl.ds(i * load, load)
        loads.append(pltpu.make_async_copy(x_ref.at[at], x.at[at], load_sem.at[i]))
        loads[-1].start()

    barrier = pltpu.get_barrier_semaphore()

    def greet(**where):
        pl.semaphore_signal(barrier, inc=1, device_id=where, device_id_type=MESH)

    for other in others:
        greet(row=other)

    @pl.when(not_first)
    def _():
        greet(pair=p - 1)

    @pl.when(not_last)
    def _():
        greet(pair=p + 1)

    @pl.when(ends)
    def _():
        greet(pair=seam - 1)
        greet(pair=seam)
        pl.semaphore_wait(barrier, 6)

    @pl.when(middle)
    def _():
        greet(pair=0)
        greet(pair=n_pair - 1)
        pl.semaphore_wait(barrier, 7)

    @pl.when(jnp.logical_not(jnp.logical_or(ends, middle)))
    def _():
        pl.semaphore_wait(barrier, 5)

    def send(src, dst, send_sem, recv_sem, **where):
        return pltpu.make_async_remote_copy(
            src_ref=src, dst_ref=dst, send_sem=send_sem, recv_sem=recv_sem, device_id=where, device_id_type=MESH
        )

    def raw_copy(side, **where):
        return send(x_ref.at[pl.ds(main, early)], raw.at[side], raw_send.at[side], raw_recv.at[side], **where)

    @pl.when(rightward)
    def _():
        raw_copy(0, pair=p + 1).start()

    @pl.when(leftward)
    def _():
        raw_copy(1, pair=p - 1).start()

    def add_gram(tops, bots, fresh):
        cross = inner(split(tops), split(bots))
        one, two = column_sums(tops), column_sums(bots)
        if fresh:
            acc[...] = cross
            sums[0] = one
            sums[1] = two
        else:
            acc[...] += cross
            sums[0] += one
            sums[1] += two

    size = width // 2
    step = size // PIECES

    def piece(k):
        return pl.ds(k * step, step + (EXTRA if k == PIECES - 1 else 0))

    def row_copies(turn, k):
        def along(src, dst, stage, other):
            return send(src, dst, row_send.at[turn, stage, k], row_recv.at[turn, stage, k], row=other)

        return (
            along(part.at[turn, 1 - core, piece(k)], got.at[turn, 0, piece(k)], 0, mate),
            along(part.at[turn, core, piece(k)], got.at[turn, 1, piece(k)], 1, across),
            along(full.at[turn, core, piece(k)], full.at[turn, core, piece(k)], 2, mate),
        )

    def row_sum(turn):
        for h in range(2):
            part[turn, h, pl.ds(0, size)] = acc[pl.ds(h * size, size)]
            part[turn, h, pl.ds(size, EXTRA)] = sums[h]
        copies = [row_copies(turn, k) for k in range(PIECES)]
        for one, _, _ in copies:
            one.start()
        for k, (one, two, _) in enumerate(copies):
            one.wait_recv()
            part[turn, core, piece(k)] += got[turn, 0, piece(k)]
            two.start()
        for k, (_, two, three) in enumerate(copies):
            two.wait_recv()
            full[turn, core, piece(k)] = part[turn, core, piece(k)] + got[turn, 1, piece(k)]
            three.start()
        for _, _, three in copies:
            three.wait_recv()
        cross = jnp.concatenate([full[turn, 0, pl.ds(0, size)], full[turn, 1, pl.ds(0, size)]], axis=0)
        diag = [jnp.sum(full[turn, h, pl.ds(size, EXTRA)], axis=0, keepdims=True) for h in range(2)]
        return angles(cross, *diag)

    for i in range(samples // load):
        loads[i].wait()
        at = pl.ds(i * load, load)
        add_gram(x[at, :width], x[at, width:], i == 0)

    theta = row_sum(0)
    theta_own[...] = theta

    def quarter(of):
        return pl.ds(pl.multiple_of(of * (width // 4), width // 4), width // 4)

    def theta_copy(side, q, **where):
        at = quarter((row, across)[q])
        return send(theta_own.at[at], thetas.at[side, at], theta_send.at[side, q], theta_recv.at[side, q], **where)

    @pl.when(rightward)
    def _():
        theta_copy(0, 0, pair=p + 1).start()

    @pl.when(leftward)
    def _():
        theta_copy(1, 0, pair=p - 1).start()

    @pl.when(p == n_pair - 2)
    def _():
        theta_copy(0, 1, pair=p + 1).start()

    @pl.when(p == 1)
    def _():
        theta_copy(1, 1, pair=p - 1).start()

    write_turn(theta, turn_high, turn_low)

    def rows_of(i):
        return pl.ds(pl.multiple_of(i * chunk, chunk), chunk)

    def to(half, side, i, **where):
        return send(
            out.at[half, rows_of(i)], pair_ref.at[rows_of(i), halves[side]],
            send_sem.at[side, i], recv_sem.at[side, i], **where,
        )

    def keep(side, i):
        return pltpu.make_async_copy(out.at[0, rows_of(i)], pair_ref.at[rows_of(i), halves[side]], recv_sem.at[side, i])

    def rotate(i, carry):
        at = rows_of(i)
        value = split(x[at])
        top, bot = (dot3(value, (turn_high[h], turn_low[h])) for h in range(2))
        out[0, at] = top
        out[1, at] = bot

        @pl.when(first)
        def _():
            to(1, 0, i, pair=p + 1).start()
            keep(0, i).start()

        @pl.when(jnp.logical_and(not_first, not_last))
        def _():
            to(0, 0, i, pair=p + 1).start()

        @pl.when(not_first)
        def _():
            to(1, 1, i, pair=p - 1).start()

        @pl.when(last)
        def _():
            keep(1, i).start()

        return carry

    end = pl.ds(main, early)

    def hop(k, src, dst, **where):
        return send(src, dst, relay_send.at[k], relay_recv.at[k], **where)

    def hop_out(**where):
        return hop(0, relay.at[0], relay.at[1], **where)

    def hop_on(side, **where):
        return hop(1, relay.at[1], pair_ref.at[end, halves[side]], **where)

    for half, here, there in ((0, before, n_pair - 1), (1, after, 0)):

        @pl.when(here)
        def _(half=half, there=there):
            relay[0] = dot3(split(x[end]), (turn_high[half], turn_low[half]))
            hop_out(pair=there).start()

    lax.fori_loop(0, n_chunks, rotate, 0)

    for side, here, there in ((0, last, seam), (1, first, seam - 1)):

        @pl.when(here)
        def _(side=side, there=there):
            hop_out(pair=there).wait_recv()
            hop_on(side, pair=there).start()

    def share(side, k, q, of):
        at = quarter(of)
        return send(thetas.at[side, at], thetas.at[side, at], share_send.at[side, k + q], share_recv.at[side, k + q], row=others[k])

    edge = (first, last)
    wide = (last, first)
    narrow = tuple(jnp.logical_and(inside[side], jnp.logical_not(wide[side])) for side in range(2))
    for side in range(2):

        @pl.when(narrow[side])
        def _(side=side):
            theta_copy(side, 0, pair=p).wait_recv()
            for k in range(3):
                share(side, k, 0, row).start()

        @pl.when(wide[side])
        def _(side=side):
            for q in range(2):
                theta_copy(side, q, pair=p).wait_recv()
                share(side, 0, q, (row, across)[q]).start()

        @pl.when(edge[side])
        def _(side=side):
            thetas[side] = theta_own[...]
            raw[side] = x[end]

    for side in range(2):

        @pl.when(narrow[side])
        def _(side=side):
            for k in range(3):
                share(side, k, 0, others[k]).wait_recv()

        @pl.when(wide[side])
        def _(side=side):
            for q in range(2):
                share(side, 0, q, (mate, 3 - row)[q]).wait_recv()

        @pl.when(inside[side])
        def _(side=side):
            raw_copy(side, pair=p).wait_recv()

        @pl.when((after, before)[side])
        def _(side=side):
            hop_on(side, pair=p).wait_recv()

        @pl.when(jnp.logical_not((after, before)[side]))
        def _(side=side):
            write_turn(thetas[side], early_high, early_low)
            half = (p == 1).astype(jnp.int32) if side == 0 else not_last.astype(jnp.int32)
            pair_ref[end, halves[side]] = dot3(split(raw[side]), (early_high[half], early_low[half]))

    add_gram(pair_ref[end, halves[0]], pair_ref[end, halves[1]], True)

    def receive(i, carry):
        keep(0, i).wait()
        keep(1, i).wait()

        at = rows_of(i)
        add_gram(pair_ref[at, halves[0]], pair_ref[at, halves[1]], False)
        return carry

    lax.fori_loop(0, n_chunks, receive, 0)
    write_turn(row_sum(1), high_ref, low_ref)

    def finish(i, carry):
        @pl.when(not_last)
        def _():
            to(0, 0, i, pair=p + 1).wait_send()

        @pl.when(not_first)
        def _():
            to(1, 1, i, pair=p - 1).wait_send()

        return carry

    lax.fori_loop(0, n_chunks, finish, 0)
    for turn in range(2):
        for k in range(PIECES):
            for copy in row_copies(turn, k):
                copy.wait_send()
    for side, goes, twice in ((0, rightward, p == n_pair - 2), (1, leftward, p == 1)):

        @pl.when(goes)
        def _(side=side):
            theta_copy(side, 0, pair=p).wait_send()
            raw_copy(side, pair=p).wait_send()

        @pl.when(twice)
        def _(side=side):
            theta_copy(side, 1, pair=p).wait_send()

        @pl.when(narrow[side])
        def _(side=side):
            for k in range(3):
                share(side, k, 0, row).wait_send()

        @pl.when(wide[side])
        def _(side=side):
            for q in range(2):
                share(side, 0, q, (row, across)[q]).wait_send()
            hop_on(side, pair=p).wait_send()

    @pl.when(middle)
    def _():
        hop_out(pair=p).wait_send()


def rotate_kernel(tiles, x_ref, high_ref, low_ref, out_ref, out, sem):
    copies = []
    at = 0
    for k, rows in enumerate(tiles):
        part = pl.ds(at, rows)
        value = split(x_ref[part])
        out[part] = jnp.concatenate([dot3(value, (high_ref[h], low_ref[h])) for h in range(2)], axis=1)
        copies.append(pltpu.make_async_copy(out.at[part], out_ref.at[part], sem.at[k]))
        copies[-1].start()
        at += rows
    for copy in copies:
        copy.wait()


def shards(n_pair, states):
    samples, both = states.shape
    width = both // 2
    chunk = 128
    load = 256
    early = 256
    main = samples - early
    n_chunks = main // chunk
    turn = (2, both, width)
    pair, high, low = pl.pallas_call(
        functools.partial(exchange_kernel, n_pair, chunk, load, early),
        out_shape=[pltpu.VMEM((samples, both), F32), pltpu.VMEM(turn, BF16), pltpu.VMEM(turn, BF16)],
        in_specs=[pl.BlockSpec(memory_space=pltpu.HBM)],
        out_specs=[pl.BlockSpec(memory_space=pltpu.VMEM)] * 3,
        scratch_shapes=[
            pltpu.VMEM((samples, both), F32),
            pltpu.VMEM((2, main, width), F32),
            pltpu.VMEM((2, early, both), F32),
            pltpu.VMEM((2, 2, width // 2 + EXTRA, width), F32),
            pltpu.VMEM((2, 2, width // 2 + EXTRA, width), F32),
            pltpu.VMEM((2, 2, width // 2 + EXTRA, width), F32),
            pltpu.VMEM((width, width), F32),
            pltpu.VMEM((2, EXTRA, width), F32),
            pltpu.VMEM((width, width), F32),
            pltpu.VMEM((2, width, width), F32),
            pltpu.VMEM(turn, BF16),
            pltpu.VMEM(turn, BF16),
            pltpu.VMEM(turn, BF16),
            pltpu.VMEM(turn, BF16),
            pltpu.VMEM((2, early, width), F32),
            pltpu.SemaphoreType.DMA((samples // load,)),
            pltpu.SemaphoreType.DMA((2, n_chunks)),
            pltpu.SemaphoreType.DMA((2, n_chunks)),
            pltpu.SemaphoreType.DMA((2,)),
            pltpu.SemaphoreType.DMA((2,)),
            pltpu.SemaphoreType.DMA((2, 2)),
            pltpu.SemaphoreType.DMA((2, 2)),
            pltpu.SemaphoreType.DMA((2, 3)),
            pltpu.SemaphoreType.DMA((2, 3)),
            pltpu.SemaphoreType.DMA((2, 3, PIECES)),
            pltpu.SemaphoreType.DMA((2, 3, PIECES)),
            pltpu.SemaphoreType.DMA((2,)),
            pltpu.SemaphoreType.DMA((2,)),
        ],
        compiler_params=pltpu.CompilerParams(
            collective_id=0, has_side_effects=True, vmem_limit_bytes=40 * 2**20
        ),
        name="exchange",
    )(pltpu.with_memory_space_constraint(states, pltpu.HBM))
    tiles = (512, 512, 512, 256, 256)
    return pl.pallas_call(
        functools.partial(rotate_kernel, tiles),
        out_shape=jax.ShapeDtypeStruct((samples, both), F32),
        in_specs=[pl.BlockSpec(memory_space=pltpu.VMEM)] * 3,
        out_specs=pl.BlockSpec(memory_space=pltpu.HBM),
        scratch_shapes=[pltpu.VMEM((samples, both), F32), pltpu.SemaphoreType.DMA((len(tiles),))],
        compiler_params=pltpu.CompilerParams(vmem_limit_bytes=20 * 2**20),
        name="rotate",
    )(pair, high, low)


def solution(mesh):
    spec = P("row", "pair")
    return jax.shard_map(
        functools.partial(shards, mesh.shape["pair"]),
        mesh=mesh, in_specs=(spec,), out_specs=spec, check_vma=False,
    )
```

```python
import functools

import jax
import jax.numpy as jnp
from jax import lax
from jax.experimental import pallas as pl
from jax.experimental.pallas import tpu as pltpu
from jax.sharding import PartitionSpec as P

MESH = pl.DeviceIdType.MESH
F32 = jnp.float32
BF16 = jnp.bfloat16
EXTRA = 8
PIECES = 2
MEET = 1


def split(value):
    high = value.astype(BF16)
    return high, (value - high.astype(F32)).astype(BF16)


def dot(left, right, dims):
    return lax.dot_general(left, right, (dims, ((), ())), preferred_element_type=F32)


def dot3(left, right, dims=((1,), (0,))):
    lh, ll = left
    rh, rl = right
    return dot(lh, rh, dims) + (dot(lh, rl, dims) + dot(ll, rh, dims))


def inner(left, right):
    return dot3(left, right, ((0,), (0,)))


def column_sums(value):
    rows, width = value.shape
    return jnp.sum((value * value).reshape(rows // EXTRA, EXTRA, width), axis=0)


def angles(cross, first, second):
    width = cross.shape[0]
    first = jnp.broadcast_to(first, (width, width)).T
    second = jnp.broadcast_to(second, (width, width))
    gap = second - first
    raw = cross * gap / (gap * gap + first * second + 1e-06)
    total = jnp.sum(jnp.sum(raw * raw, axis=0, keepdims=True), axis=1, keepdims=True)
    return raw / (1.0 + jnp.sqrt(total))


def polynomial(square, ident):
    halves = split(square)
    second = dot3(halves, halves)
    factor = 0.375 * ident - 0.3125 * square + 0.0625 * second
    return ident - 0.5 * square + dot3(split(second), split(factor))


def write_turn(theta, high_ref, low_ref):
    width = theta.shape[0]
    rows = lax.broadcasted_iota(jnp.int32, (width, width), 0)
    cols = lax.broadcasted_iota(jnp.int32, (width, width), 1)
    ident = jnp.where(rows == cols, 1.0, 0.0).astype(F32)
    plain = split(theta)
    flipped = split(theta.T)
    upper = polynomial(dot3(plain, flipped), ident)
    lower = polynomial(dot3(flipped, plain), ident)
    off = dot3(split(upper), plain)
    one, two = pl.ds(0, width), pl.ds(width, width)
    for half, at, block in ((0, one, upper), (1, one, off), (0, two, -off.T), (1, two, lower)):
        high, low = split(block)
        high_ref[half, at] = high
        low_ref[half, at] = low


def exchange_kernel(
    n_pair, chunk, load, early, extra,
    x_ref, pair_ref, high_ref, low_ref,
    x, out, raw, part, got, full, acc, sums, theta_own, thetas, turn_high, turn_low, early_high, early_low, relay,
    load_sem, send_sem, recv_sem, raw_send, raw_recv, theta_send, theta_recv, share_send, share_recv, row_send, row_recv,
    relay_send, relay_recv, far,
):
    p = lax.axis_index("pair")
    row = lax.axis_index("row")
    core = lax.rem(row, 2)
    mate = row + 1 - 2 * core
    across = lax.rem(row + 2, 4)
    others = (mate, across, 3 - row)
    samples, both = x.shape
    width = both // 2
    main = samples - early
    n_chunks = main // chunk
    n_direct = n_chunks - extra // chunk
    n_hops = (early + extra) // chunk
    first = p == 0
    last = p == n_pair - 1
    not_first = jnp.logical_not(first)
    not_last = jnp.logical_not(last)
    seam = n_pair // 2
    before = p == seam - 1
    after = p == seam
    ends = jnp.logical_or(first, last)
    middle = jnp.logical_or(before, after)
    rightward = jnp.logical_and(not_last, jnp.logical_not(before))
    leftward = jnp.logical_and(not_first, jnp.logical_not(after))
    inside = (jnp.logical_and(not_first, jnp.logical_not(after)), jnp.logical_and(not_last, jnp.logical_not(before)))
    halves = pl.ds(0, width), pl.ds(width, width)

    loads = []
    for i in range(samples // load):
        at = pl.ds(i * load, load)
        loads.append(pltpu.make_async_copy(x_ref.at[at], x.at[at], load_sem.at[i]))
        loads[-1].start()

    barrier = pltpu.get_barrier_semaphore()

    def greet(**where):
        pl.semaphore_signal(barrier, inc=1, device_id=where, device_id_type=MESH)

    for other in others:
        greet(row=other)

    def meet():
        @pl.when(jnp.logical_and(not_first, jnp.logical_not(after)))
        def _():
            greet(pair=p - 1)

        @pl.when(jnp.logical_and(not_last, jnp.logical_not(before)))
        def _():
            greet(pair=p + 1)

        @pl.when(first)
        def _():
            greet(pair=seam - 1)
            greet(pair=seam)

        @pl.when(last)
        def _():
            greet(pair=seam - 1)

        @pl.when(after)
        def _():
            greet(pair=seam - 1)
            greet(pair=n_pair - 1)

    meet()

    def met():
        @pl.when(first)
        def _():
            pl.semaphore_wait(barrier, 4)

        @pl.when(before)
        def _():
            pl.semaphore_wait(barrier, 7)
            for there in (0, seam):
                pl.semaphore_signal(far, inc=1, device_id={"pair": there}, device_id_type=MESH)

        @pl.when(jnp.logical_not(jnp.logical_or(first, before)))
        def _():
            pl.semaphore_wait(barrier, 5)

    def send(src, dst, send_sem, recv_sem, **where):
        return pltpu.make_async_remote_copy(
            src_ref=src, dst_ref=dst, send_sem=send_sem, recv_sem=recv_sem, device_id=where, device_id_type=MESH
        )

    def raw_copy(side, **where):
        return send(x_ref.at[pl.ds(main, early)], raw.at[side], raw_send.at[side], raw_recv.at[side], **where)

    def raw_start():
        @pl.when(rightward)
        def _():
            raw_copy(0, pair=p + 1).start()

        @pl.when(leftward)
        def _():
            raw_copy(1, pair=p - 1).start()

    def add_gram(tops, bots, fresh):
        cross = inner(split(tops), split(bots))
        one, two = column_sums(tops), column_sums(bots)
        if fresh:
            acc[...] = cross
            sums[0] = one
            sums[1] = two
        else:
            acc[...] += cross
            sums[0] += one
            sums[1] += two

    size = width // 2
    step = size // PIECES

    def piece(k):
        return pl.ds(k * step, step + (EXTRA if k == PIECES - 1 else 0))

    def row_copies(turn, k):
        def along(src, dst, stage, other):
            return send(src, dst, row_send.at[turn, stage, k], row_recv.at[turn, stage, k], row=other)

        return (
            along(part.at[turn, 1 - core, piece(k)], got.at[turn, 0, piece(k)], 0, mate),
            along(part.at[turn, core, piece(k)], got.at[turn, 1, piece(k)], 1, across),
            along(full.at[turn, core, piece(k)], full.at[turn, core, piece(k)], 2, mate),
        )

    def row_sum(turn):
        for h in range(2):
            part[turn, h, pl.ds(0, size)] = acc[pl.ds(h * size, size)]
            part[turn, h, pl.ds(size, EXTRA)] = sums[h]
        copies = [row_copies(turn, k) for k in range(PIECES)]
        for one, _, _ in copies:
            one.start()
        for k, (one, two, _) in enumerate(copies):
            one.wait_recv()
            part[turn, core, piece(k)] += got[turn, 0, piece(k)]
            two.start()
        for k, (_, two, three) in enumerate(copies):
            two.wait_recv()
            full[turn, core, piece(k)] = part[turn, core, piece(k)] + got[turn, 1, piece(k)]
            three.start()
        for _, _, three in copies:
            three.wait_recv()
        cross = jnp.concatenate([full[turn, 0, pl.ds(0, size)], full[turn, 1, pl.ds(0, size)]], axis=0)
        diag = [jnp.sum(full[turn, h, pl.ds(size, EXTRA)], axis=0, keepdims=True) for h in range(2)]
        return angles(cross, *diag)

    for i in range(samples // load):
        loads[i].wait()
        at = pl.ds(i * load, load)
        add_gram(x[at, :width], x[at, width:], i == 0)
        if i == MEET:
            met()
            raw_start()

    theta = row_sum(0)
    theta_own[...] = theta

    def quarter(of):
        return pl.ds(pl.multiple_of(of * (width // 4), width // 4), width // 4)

    def theta_copy(side, q, **where):
        at = quarter((row, across)[q])
        return send(theta_own.at[at], thetas.at[side, at], theta_send.at[side, q], theta_recv.at[side, q], **where)

    @pl.when(rightward)
    def _():
        theta_copy(0, 0, pair=p + 1).start()

    @pl.when(leftward)
    def _():
        theta_copy(1, 0, pair=p - 1).start()

    @pl.when(p == n_pair - 2)
    def _():
        theta_copy(0, 1, pair=p + 1).start()

    @pl.when(p == 1)
    def _():
        theta_copy(1, 1, pair=p - 1).start()

    write_turn(theta, turn_high, turn_low)

    def rows_of(i):
        return pl.ds(pl.multiple_of(i * chunk, chunk), chunk)

    def to(half, side, i, **where):
        return send(
            out.at[half, rows_of(i)], pair_ref.at[rows_of(i), halves[side]],
            send_sem.at[side, i], recv_sem.at[side, i], **where,
        )

    def keep(side, i):
        return pltpu.make_async_copy(out.at[0, rows_of(i)], pair_ref.at[rows_of(i), halves[side]], recv_sem.at[side, i])

    def goes_right(i):
        return jnp.logical_and(not_last, jnp.logical_or(jnp.logical_not(before), i < n_direct))

    def goes_left(i):
        return jnp.logical_and(not_first, jnp.logical_or(jnp.logical_not(after), i < n_direct))

    def rotate(i, carry):
        at = rows_of(i)
        value = split(x[at])
        top, bot = (dot3(value, (turn_high[h], turn_low[h])) for h in range(2))
        out[0, at] = top
        out[1, at] = bot

        @pl.when(first)
        def _():
            to(1, 0, i, pair=p + 1).start()
            keep(0, i).start()

        @pl.when(jnp.logical_and(not_first, goes_right(i)))
        def _():
            to(0, 0, i, pair=p + 1).start()

        @pl.when(goes_left(i))
        def _():
            to(1, 1, i, pair=p - 1).start()

        @pl.when(last)
        def _():
            keep(1, i).start()

        return carry

    end = pl.ds(main, early)

    def hop(stage, k, src, dst, **where):
        return send(src, dst, relay_send.at[stage, k], relay_recv.at[stage, k], **where)

    def hop_out(k, **where):
        at = pl.ds(k * chunk, chunk)
        return hop(0, k, relay.at[0, at], relay.at[1, at], **where)

    def hop_on(side, k, **where):
        to_rows = pl.ds(samples - early - extra + k * chunk, chunk)
        return hop(1, k, relay.at[1, pl.ds(k * chunk, chunk)], pair_ref.at[to_rows, halves[side]], **where)

    @pl.when(after)
    def _():
        pl.semaphore_wait(far, 1)

    for half, here, there in ((0, before, n_pair - 1), (1, after, 0)):

        @pl.when(here)
        def _(half=half, there=there):
            for k in range(n_hops):
                value = split(x[pl.ds(samples - early - extra + k * chunk, chunk)])
                relay[0, pl.ds(k * chunk, chunk)] = dot3(value, (turn_high[half], turn_low[half]))
                hop_out(k, pair=there).start()

    lax.fori_loop(0, n_chunks, rotate, 0)

    for side, here, there in ((0, last, seam), (1, first, seam - 1)):

        @pl.when(here)
        def _(side=side, there=there):
            if side == 1:
                pl.semaphore_wait(far, 1)
            for k in range(n_hops):
                hop_out(k, pair=there).wait_recv()
                hop_on(side, k, pair=there).start()

    def share(side, k, q, of):
        at = quarter(of)
        return send(thetas.at[side, at], thetas.at[side, at], share_send.at[side, k + q], share_recv.at[side, k + q], row=others[k])

    edge = (first, last)
    wide = (last, first)
    narrow = tuple(jnp.logical_and(inside[side], jnp.logical_not(wide[side])) for side in range(2))
    for side in range(2):

        @pl.when(narrow[side])
        def _(side=side):
            theta_copy(side, 0, pair=p).wait_recv()
            for k in range(3):
                share(side, k, 0, row).start()

        @pl.when(wide[side])
        def _(side=side):
            for q in range(2):
                theta_copy(side, q, pair=p).wait_recv()
                share(side, 0, q, (row, across)[q]).start()

        @pl.when(edge[side])
        def _(side=side):
            thetas[side] = theta_own[...]
            raw[side] = x[end]

    for side in range(2):

        @pl.when(narrow[side])
        def _(side=side):
            for k in range(3):
                share(side, k, 0, others[k]).wait_recv()

        @pl.when(wide[side])
        def _(side=side):
            for q in range(2):
                share(side, 0, q, (mate, 3 - row)[q]).wait_recv()

        @pl.when(inside[side])
        def _(side=side):
            raw_copy(side, pair=p).wait_recv()

        @pl.when(jnp.logical_not((after, before)[side]))
        def _(side=side):
            write_turn(thetas[side], early_high, early_low)
            half = (p == 1).astype(jnp.int32) if side == 0 else not_last.astype(jnp.int32)
            pair_ref[end, halves[side]] = dot3(split(raw[side]), (early_high[half], early_low[half]))

    acc[...] = jnp.zeros_like(acc)
    sums[...] = jnp.zeros_like(sums)

    def receive(i, carry):
        @pl.when(jnp.logical_or(jnp.logical_not(after), i < n_direct))
        def _():
            keep(0, i).wait()

        @pl.when(jnp.logical_or(jnp.logical_not(before), i < n_direct))
        def _():
            keep(1, i).wait()

        @pl.when(i == n_direct)
        def _():
            for side in range(2):

                @pl.when((after, before)[side])
                def _(side=side):
                    for k in range(n_hops):
                        hop_on(side, k, pair=p).wait_recv()

            add_gram(pair_ref[end, halves[0]], pair_ref[end, halves[1]], False)


        at = rows_of(i)
        add_gram(pair_ref[at, halves[0]], pair_ref[at, halves[1]], False)
        return carry

    lax.fori_loop(0, n_chunks, receive, 0)
    write_turn(row_sum(1), high_ref, low_ref)

    def finish(i, carry):
        @pl.when(goes_right(i))
        def _():
            to(0, 0, i, pair=p + 1).wait_send()

        @pl.when(goes_left(i))
        def _():
            to(1, 1, i, pair=p - 1).wait_send()

        return carry

    lax.fori_loop(0, n_chunks, finish, 0)
    for turn in range(2):
        for k in range(PIECES):
            for copy in row_copies(turn, k):
                copy.wait_send()
    for side, goes, twice in ((0, rightward, p == n_pair - 2), (1, leftward, p == 1)):

        @pl.when(goes)
        def _(side=side):
            theta_copy(side, 0, pair=p).wait_send()
            raw_copy(side, pair=p).wait_send()

        @pl.when(twice)
        def _(side=side):
            theta_copy(side, 1, pair=p).wait_send()

        @pl.when(narrow[side])
        def _(side=side):
            for k in range(3):
                share(side, k, 0, row).wait_send()

        @pl.when(wide[side])
        def _(side=side):
            for q in range(2):
                share(side, 0, q, (row, across)[q]).wait_send()
            for k in range(n_hops):
                hop_on(side, k, pair=p).wait_send()

    @pl.when(middle)
    def _():
        for k in range(n_hops):
            hop_out(k, pair=p).wait_send()


def rotate_kernel(tiles, x_ref, high_ref, low_ref, out_ref, out, sem):
    copies = []
    at = 0
    for k, rows in enumerate(tiles):
        part = pl.ds(at, rows)
        value = split(x_ref[part])
        out[part] = jnp.concatenate([dot3(value, (high_ref[h], low_ref[h])) for h in range(2)], axis=1)
        copies.append(pltpu.make_async_copy(out.at[part], out_ref.at[part], sem.at[k]))
        copies[-1].start()
        at += rows
    for copy in copies:
        copy.wait()


def shards(n_pair, states):
    samples, both = states.shape
    width = both // 2
    chunk = 128
    load = 256
    early = 256
    extra = 256
    main = samples - early
    n_chunks = main // chunk
    turn = (2, both, width)
    pair, high, low = pl.pallas_call(
        functools.partial(exchange_kernel, n_pair, chunk, load, early, extra),
        out_shape=[pltpu.VMEM((samples, both), F32), pltpu.VMEM(turn, BF16), pltpu.VMEM(turn, BF16)],
        in_specs=[pl.BlockSpec(memory_space=pltpu.HBM)],
        out_specs=[pl.BlockSpec(memory_space=pltpu.VMEM)] * 3,
        scratch_shapes=[
            pltpu.VMEM((samples, both), F32),
            pltpu.VMEM((2, main, width), F32),
            pltpu.VMEM((2, early, both), F32),
            pltpu.VMEM((2, 2, width // 2 + EXTRA, width), F32),
            pltpu.VMEM((2, 2, width // 2 + EXTRA, width), F32),
            pltpu.VMEM((2, 2, width // 2 + EXTRA, width), F32),
            pltpu.VMEM((width, width), F32),
            pltpu.VMEM((2, EXTRA, width), F32),
            pltpu.VMEM((width, width), F32),
            pltpu.VMEM((2, width, width), F32),
            pltpu.VMEM(turn, BF16),
            pltpu.VMEM(turn, BF16),
            pltpu.VMEM(turn, BF16),
            pltpu.VMEM(turn, BF16),
            pltpu.VMEM((2, early + extra, width), F32),
            pltpu.SemaphoreType.DMA((samples // load,)),
            pltpu.SemaphoreType.DMA((2, n_chunks)),
            pltpu.SemaphoreType.DMA((2, n_chunks)),
            pltpu.SemaphoreType.DMA((2,)),
            pltpu.SemaphoreType.DMA((2,)),
            pltpu.SemaphoreType.DMA((2, 2)),
            pltpu.SemaphoreType.DMA((2, 2)),
            pltpu.SemaphoreType.DMA((2, 3)),
            pltpu.SemaphoreType.DMA((2, 3)),
            pltpu.SemaphoreType.DMA((2, 3, PIECES)),
            pltpu.SemaphoreType.DMA((2, 3, PIECES)),
            pltpu.SemaphoreType.DMA((2, (early + extra) // chunk)),
            pltpu.SemaphoreType.DMA((2, (early + extra) // chunk)),
            pltpu.SemaphoreType.REGULAR,
        ],
        compiler_params=pltpu.CompilerParams(
            collective_id=0, has_side_effects=True, vmem_limit_bytes=40 * 2**20
        ),
        name="exchange",
    )(pltpu.with_memory_space_constraint(states, pltpu.HBM))
    tiles = (512, 512, 512, 256, 256)
    return pl.pallas_call(
        functools.partial(rotate_kernel, tiles),
        out_shape=jax.ShapeDtypeStruct((samples, both), F32),
        in_specs=[pl.BlockSpec(memory_space=pltpu.VMEM)] * 3,
        out_specs=pl.BlockSpec(memory_space=pltpu.HBM),
        scratch_shapes=[pltpu.VMEM((samples, both), F32), pltpu.SemaphoreType.DMA((len(tiles),))],
        compiler_params=pltpu.CompilerParams(vmem_limit_bytes=20 * 2**20),
        name="rotate",
    )(pair, high, low)


def solution(mesh):
    spec = P("row", "pair")
    return jax.shard_map(
        functools.partial(shards, mesh.shape["pair"]),
        mesh=mesh, in_specs=(spec,), out_specs=spec, check_vma=False,
    )
```

```python
import functools

import jax
import jax.numpy as jnp
from jax import lax
from jax.experimental import pallas as pl
from jax.experimental.pallas import tpu as pltpu
from jax.sharding import PartitionSpec as P

MESH = pl.DeviceIdType.MESH
F32 = jnp.float32
BF16 = jnp.bfloat16
EXTRA = 8
PIECES = 1


def split(value):
    high = value.astype(BF16)
    return high, (value - high.astype(F32)).astype(BF16)


def dot(left, right, dims):
    return lax.dot_general(left, right, (dims, ((), ())), preferred_element_type=F32)


def dot3(left, right, dims=((1,), (0,))):
    lh, ll = left
    rh, rl = right
    return dot(lh, rh, dims) + (dot(lh, rl, dims) + dot(ll, rh, dims))


def inner(left, right):
    return dot3(left, right, ((0,), (0,)))


def column_sums(value):
    rows, width = value.shape
    return jnp.sum((value * value).reshape(rows // EXTRA, EXTRA, width), axis=0)


def angles(cross, first, second):
    width = cross.shape[0]
    first = jnp.broadcast_to(first, (width, width)).T
    second = jnp.broadcast_to(second, (width, width))
    gap = second - first
    raw = cross * gap / (gap * gap + first * second + 1e-06)
    total = jnp.sum(jnp.sum(raw * raw, axis=0, keepdims=True), axis=1, keepdims=True)
    return raw, 1.0 / (1.0 + jnp.sqrt(total))


def polynomial(square, ident):
    halves = split(square)
    second = dot3(halves, halves)
    factor = 0.375 * ident - 0.3125 * square + 0.0625 * second
    return ident - 0.5 * square + dot3(split(second), split(factor))


def write_turn(theta, scale, high_ref, low_ref):
    width = theta.shape[0]
    rows = lax.broadcasted_iota(jnp.int32, (width, width), 0)
    cols = lax.broadcasted_iota(jnp.int32, (width, width), 1)
    ident = jnp.where(rows == cols, 1.0, 0.0).astype(F32)
    plain = split(theta)
    flipped = split(theta.T)
    upper = polynomial(dot3(plain, flipped) * (scale * scale), ident)
    lower = polynomial(dot3(flipped, plain) * (scale * scale), ident)
    off = dot3(split(upper), plain) * scale
    one, two = pl.ds(0, width), pl.ds(width, width)
    for half, at, block in ((0, one, upper), (1, one, off), (0, two, -off.T), (1, two, lower)):
        high, low = split(block)
        high_ref[half, at] = high
        low_ref[half, at] = low


def exchange_kernel(
    n_pair, chunk, load, early, extra,
    x_ref, pair_ref, high_ref, low_ref,
    x, out, raw, part, got, full, theta_own, thetas, turn_high, turn_low, early_high, early_low, relay,
    load_sem, send_sem, recv_sem, raw_send, raw_recv, theta_send, theta_recv, share_send, share_recv, row_send, row_recv,
    relay_send, relay_recv, far,
):
    p = lax.axis_index("pair")
    row = lax.axis_index("row")
    core = lax.rem(row, 2)
    mate = row + 1 - 2 * core
    across = lax.rem(row + 2, 4)
    others = (mate, across, 3 - row)
    samples, both = x.shape
    width = both // 2
    main = samples - early
    n_chunks = main // chunk
    n_direct = n_chunks - extra // chunk
    n_hops = (early + extra) // chunk
    first = p == 0
    last = p == n_pair - 1
    not_first = jnp.logical_not(first)
    not_last = jnp.logical_not(last)
    seam = n_pair // 2
    before = p == seam - 1
    after = p == seam
    ends = jnp.logical_or(first, last)
    middle = jnp.logical_or(before, after)
    rightward = jnp.logical_and(not_last, jnp.logical_not(before))
    leftward = jnp.logical_and(not_first, jnp.logical_not(after))
    inside = (jnp.logical_and(not_first, jnp.logical_not(after)), jnp.logical_and(not_last, jnp.logical_not(before)))
    halves = pl.ds(0, width), pl.ds(width, width)

    loads = []
    for i in range(samples // load):
        at = pl.ds(i * load, load)
        loads.append(pltpu.make_async_copy(x_ref.at[at], x.at[at], load_sem.at[i]))
        loads[-1].start()

    barrier = pltpu.get_barrier_semaphore()

    def greet(**where):
        pl.semaphore_signal(barrier, inc=1, device_id=where, device_id_type=MESH)

    for other in others:
        greet(row=other)

    def meet():
        @pl.when(jnp.logical_and(not_first, jnp.logical_not(after)))
        def _():
            greet(pair=p - 1)

        @pl.when(jnp.logical_and(not_last, jnp.logical_not(before)))
        def _():
            greet(pair=p + 1)

        @pl.when(first)
        def _():
            greet(pair=seam - 1)
            greet(pair=seam)

        @pl.when(last)
        def _():
            greet(pair=seam - 1)

        @pl.when(after)
        def _():
            greet(pair=seam - 1)
            greet(pair=n_pair - 1)

    meet()

    def met():
        @pl.when(first)
        def _():
            pl.semaphore_wait(barrier, 4)

        @pl.when(before)
        def _():
            pl.semaphore_wait(barrier, 7)
            for there in (0, seam):
                pl.semaphore_signal(far, inc=1, device_id={"pair": there}, device_id_type=MESH)

        @pl.when(jnp.logical_not(jnp.logical_or(first, before)))
        def _():
            pl.semaphore_wait(barrier, 5)

    def send(src, dst, send_sem, recv_sem, **where):
        return pltpu.make_async_remote_copy(
            src_ref=src, dst_ref=dst, send_sem=send_sem, recv_sem=recv_sem, device_id=where, device_id_type=MESH
        )

    def raw_copy(side, **where):
        return send(x_ref.at[pl.ds(main, early)], raw.at[side], raw_send.at[side], raw_recv.at[side], **where)

    def raw_start():
        @pl.when(rightward)
        def _():
            raw_copy(0, pair=p + 1).start()

        @pl.when(leftward)
        def _():
            raw_copy(1, pair=p - 1).start()

    size = width // 2
    step = size // PIECES

    def piece(k):
        return pl.ds(k * step, step + (EXTRA if k == PIECES - 1 else 0))

    def row_copies(turn, k):
        def along(src, dst, stage, other):
            return send(src, dst, row_send.at[turn, stage, k], row_recv.at[turn, stage, k], row=other)

        return (
            along(part.at[turn, 1 - core, piece(k)], got.at[turn, 0, piece(k)], 0, mate),
            along(part.at[turn, core, piece(k)], got.at[turn, 1, piece(k)], 1, across),
            along(full.at[turn, core, piece(k)], full.at[turn, core, piece(k)], 2, mate),
        )

    def add_half(turn, ref, at, h, fresh=False):
        left = ref[at, pl.ds(pl.multiple_of(h * size, size), size)]
        value = inner(split(left), split(ref[at, halves[1]]))
        if fresh:
            part[turn, h, pl.ds(0, size)] = value
        else:
            part[turn, h, pl.ds(0, size)] += value

    def add_sums(turn, ref, at, fresh=False):
        for h in range(2):
            value = column_sums(ref[at, halves[h]])
            if fresh:
                part[turn, h, pl.ds(size, EXTRA)] = value
            else:
                part[turn, h, pl.ds(size, EXTRA)] += value

    def add_gram(turn, ref, at):
        value = inner(split(ref[at, halves[0]]), split(ref[at, halves[1]]))
        for h in range(2):
            part[turn, h, pl.ds(0, size)] += value[h * size : (h + 1) * size]
        add_sums(turn, ref, at)

    def row_sum(turn, finish_own):
        copies = [row_copies(turn, k) for k in range(PIECES)]
        for one, _, _ in copies:
            one.start()
        finish_own()
        for k, (one, two, _) in enumerate(copies):
            one.wait_recv()
            part[turn, core, piece(k)] += got[turn, 0, piece(k)]
            two.start()
        for k, (_, two, three) in enumerate(copies):
            two.wait_recv()
            full[turn, core, piece(k)] = part[turn, core, piece(k)] + got[turn, 1, piece(k)]
            three.start()
        for _, _, three in copies:
            three.wait_recv()
        cross = jnp.concatenate([full[turn, 0, pl.ds(0, size)], full[turn, 1, pl.ds(0, size)]], axis=0)
        diag = [jnp.sum(full[turn, h, pl.ds(size, EXTRA)], axis=0, keepdims=True) for h in range(2)]
        return angles(cross, *diag)

    met()
    raw_start()
    for i in range(samples // load):
        loads[i].wait()
        at = pl.ds(i * load, load)
        add_sums(0, x, at, i == 0)
        add_half(0, x, at, 1 - core, i == 0)

    def finish_own():
        for i in range(2):
            add_half(0, x, pl.ds(i * (samples // 2), samples // 2), core, i == 0)

    raw_angles, scale = row_sum(0, finish_own)
    theta_own[...] = raw_angles * scale

    def quarter(of):
        return pl.ds(pl.multiple_of(of * (width // 4), width // 4), width // 4)

    def theta_copy(side, q, **where):
        at = quarter((row, across)[q])
        return send(theta_own.at[at], thetas.at[side, at], theta_send.at[side, q], theta_recv.at[side, q], **where)

    @pl.when(rightward)
    def _():
        theta_copy(0, 0, pair=p + 1).start()

    @pl.when(leftward)
    def _():
        theta_copy(1, 0, pair=p - 1).start()

    @pl.when(p == n_pair - 2)
    def _():
        theta_copy(0, 1, pair=p + 1).start()

    @pl.when(p == 1)
    def _():
        theta_copy(1, 1, pair=p - 1).start()

    write_turn(raw_angles, scale, turn_high, turn_low)

    def rows_of(i):
        return pl.ds(pl.multiple_of(i * chunk, chunk), chunk)

    def to(half, side, i, **where):
        return send(
            out.at[half, rows_of(i)], pair_ref.at[rows_of(i), halves[side]],
            send_sem.at[side, i], recv_sem.at[side, i], **where,
        )

    def keep(side, i):
        return pltpu.make_async_copy(out.at[0, rows_of(i)], pair_ref.at[rows_of(i), halves[side]], recv_sem.at[side, i])

    def goes_right(i):
        return jnp.logical_and(not_last, jnp.logical_or(jnp.logical_not(before), i < n_direct))

    def goes_left(i):
        return jnp.logical_and(not_first, jnp.logical_or(jnp.logical_not(after), i < n_direct))

    def rotate(i, carry):
        at = rows_of(i)
        value = split(x[at])
        top, bot = (dot3(value, (turn_high[h], turn_low[h])) for h in range(2))
        out[0, at] = top
        out[1, at] = bot

        @pl.when(first)
        def _():
            to(1, 0, i, pair=p + 1).start()
            keep(0, i).start()

        @pl.when(jnp.logical_and(not_first, goes_right(i)))
        def _():
            to(0, 0, i, pair=p + 1).start()

        @pl.when(goes_left(i))
        def _():
            to(1, 1, i, pair=p - 1).start()

        @pl.when(last)
        def _():
            keep(1, i).start()

        return carry

    end = pl.ds(main, early)

    def hop(stage, k, src, dst, **where):
        return send(src, dst, relay_send.at[stage, k], relay_recv.at[stage, k], **where)

    def hop_out(k, **where):
        at = pl.ds(k * chunk, chunk)
        return hop(0, k, relay.at[0, at], relay.at[1, at], **where)

    def hop_on(side, k, **where):
        to_rows = pl.ds(samples - early - extra + k * chunk, chunk)
        return hop(1, k, relay.at[1, pl.ds(k * chunk, chunk)], pair_ref.at[to_rows, halves[side]], **where)

    @pl.when(after)
    def _():
        pl.semaphore_wait(far, 1)

    for half, here, there in ((0, before, n_pair - 1), (1, after, 0)):

        @pl.when(here)
        def _(half=half, there=there):
            for k in range(n_hops):
                value = split(x[pl.ds(samples - early - extra + k * chunk, chunk)])
                relay[0, pl.ds(k * chunk, chunk)] = dot3(value, (turn_high[half], turn_low[half]))
                hop_out(k, pair=there).start()

    lax.fori_loop(0, n_chunks, rotate, 0)

    for side, here, there in ((0, last, seam), (1, first, seam - 1)):

        @pl.when(here)
        def _(side=side, there=there):
            if side == 1:
                pl.semaphore_wait(far, 1)
            for k in range(n_hops):
                hop_out(k, pair=there).wait_recv()
                hop_on(side, k, pair=there).start()

    def share(side, k, q, of):
        at = quarter(of)
        return send(thetas.at[side, at], thetas.at[side, at], share_send.at[side, k + q], share_recv.at[side, k + q], row=others[k])

    edge = (first, last)
    wide = (last, first)
    narrow = tuple(jnp.logical_and(inside[side], jnp.logical_not(wide[side])) for side in range(2))
    for side in range(2):

        @pl.when(narrow[side])
        def _(side=side):
            theta_copy(side, 0, pair=p).wait_recv()
            for k in range(3):
                share(side, k, 0, row).start()

        @pl.when(wide[side])
        def _(side=side):
            for q in range(2):
                theta_copy(side, q, pair=p).wait_recv()
                share(side, 0, q, (row, across)[q]).start()

        @pl.when(edge[side])
        def _(side=side):
            thetas[side] = theta_own[...]
            raw[side] = x[end]

    for side in range(2):

        @pl.when(narrow[side])
        def _(side=side):
            for k in range(3):
                share(side, k, 0, others[k]).wait_recv()

        @pl.when(wide[side])
        def _(side=side):
            for q in range(2):
                share(side, 0, q, (mate, 3 - row)[q]).wait_recv()

        @pl.when(inside[side])
        def _(side=side):
            raw_copy(side, pair=p).wait_recv()

        @pl.when(jnp.logical_not((after, before)[side]))
        def _(side=side):
            write_turn(thetas[side], 1.0, early_high, early_low)
            half = (p == 1).astype(jnp.int32) if side == 0 else not_last.astype(jnp.int32)
            pair_ref[end, halves[side]] = dot3(split(raw[side]), (early_high[half], early_low[half]))

    part[1] = jnp.zeros_like(part[1])

    def arrive(i):
        @pl.when(jnp.logical_or(jnp.logical_not(after), i < n_direct))
        def _():
            keep(0, i).wait()

        @pl.when(jnp.logical_or(jnp.logical_not(before), i < n_direct))
        def _():
            keep(1, i).wait()

        @pl.when(i == n_direct)
        def _():
            for side in range(2):

                @pl.when((after, before)[side])
                def _(side=side):
                    for k in range(n_hops):
                        hop_on(side, k, pair=p).wait_recv()

            add_gram(1, pair_ref, end)


    def receive(i, carry):
        arrive(i)
        add_gram(1, pair_ref, rows_of(i))
        return carry

    lax.fori_loop(0, n_chunks - 1, receive, 0)
    arrive(n_chunks - 1)
    tail = pl.ds((n_chunks - 1) * chunk, chunk)
    add_sums(1, pair_ref, tail)
    add_half(1, pair_ref, tail, 1 - core)
    write_turn(*row_sum(1, lambda: add_half(1, pair_ref, tail, core)), high_ref, low_ref)

    def finish(i, carry):
        @pl.when(goes_right(i))
        def _():
            to(0, 0, i, pair=p + 1).wait_send()

        @pl.when(goes_left(i))
        def _():
            to(1, 1, i, pair=p - 1).wait_send()

        return carry

    lax.fori_loop(0, n_chunks, finish, 0)
    for turn in range(2):
        for k in range(PIECES):
            for copy in row_copies(turn, k):
                copy.wait_send()
    for side, goes, twice in ((0, rightward, p == n_pair - 2), (1, leftward, p == 1)):

        @pl.when(goes)
        def _(side=side):
            theta_copy(side, 0, pair=p).wait_send()
            raw_copy(side, pair=p).wait_send()

        @pl.when(twice)
        def _(side=side):
            theta_copy(side, 1, pair=p).wait_send()

        @pl.when(narrow[side])
        def _(side=side):
            for k in range(3):
                share(side, k, 0, row).wait_send()

        @pl.when(wide[side])
        def _(side=side):
            for q in range(2):
                share(side, 0, q, (row, across)[q]).wait_send()
            for k in range(n_hops):
                hop_on(side, k, pair=p).wait_send()

    @pl.when(middle)
    def _():
        for k in range(n_hops):
            hop_out(k, pair=p).wait_send()


def rotate_kernel(tiles, x_ref, high_ref, low_ref, out_ref, out, sem):
    copies = []
    at = 0
    for k, rows in enumerate(tiles):
        part = pl.ds(at, rows)
        value = split(x_ref[part])
        out[part] = jnp.concatenate([dot3(value, (high_ref[h], low_ref[h])) for h in range(2)], axis=1)
        copies.append(pltpu.make_async_copy(out.at[part], out_ref.at[part], sem.at[k]))
        copies[-1].start()
        at += rows
    for copy in copies:
        copy.wait()


def shards(n_pair, states):
    samples, both = states.shape
    width = both // 2
    chunk = 128
    load = 512
    early = 256
    extra = 512
    main = samples - early
    n_chunks = main // chunk
    turn = (2, both, width)
    pair, high, low = pl.pallas_call(
        functools.partial(exchange_kernel, n_pair, chunk, load, early, extra),
        out_shape=[pltpu.VMEM((samples, both), F32), pltpu.VMEM(turn, BF16), pltpu.VMEM(turn, BF16)],
        in_specs=[pl.BlockSpec(memory_space=pltpu.HBM)],
        out_specs=[pl.BlockSpec(memory_space=pltpu.VMEM)] * 3,
        scratch_shapes=[
            pltpu.VMEM((samples, both), F32),
            pltpu.VMEM((2, main, width), F32),
            pltpu.VMEM((2, early, both), F32),
            pltpu.VMEM((2, 2, width // 2 + EXTRA, width), F32),
            pltpu.VMEM((2, 2, width // 2 + EXTRA, width), F32),
            pltpu.VMEM((2, 2, width // 2 + EXTRA, width), F32),
            pltpu.VMEM((width, width), F32),
            pltpu.VMEM((2, width, width), F32),
            pltpu.VMEM(turn, BF16),
            pltpu.VMEM(turn, BF16),
            pltpu.VMEM(turn, BF16),
            pltpu.VMEM(turn, BF16),
            pltpu.VMEM((2, early + extra, width), F32),
            pltpu.SemaphoreType.DMA((samples // load,)),
            pltpu.SemaphoreType.DMA((2, n_chunks)),
            pltpu.SemaphoreType.DMA((2, n_chunks)),
            pltpu.SemaphoreType.DMA((2,)),
            pltpu.SemaphoreType.DMA((2,)),
            pltpu.SemaphoreType.DMA((2, 2)),
            pltpu.SemaphoreType.DMA((2, 2)),
            pltpu.SemaphoreType.DMA((2, 3)),
            pltpu.SemaphoreType.DMA((2, 3)),
            pltpu.SemaphoreType.DMA((2, 3, PIECES)),
            pltpu.SemaphoreType.DMA((2, 3, PIECES)),
            pltpu.SemaphoreType.DMA((2, (early + extra) // chunk)),
            pltpu.SemaphoreType.DMA((2, (early + extra) // chunk)),
            pltpu.SemaphoreType.REGULAR,
        ],
        compiler_params=pltpu.CompilerParams(
            collective_id=0, has_side_effects=True, vmem_limit_bytes=40 * 2**20
        ),
        name="exchange",
    )(pltpu.with_memory_space_constraint(states, pltpu.HBM))
    tiles = (512, 512, 512, 256, 256)
    return pl.pallas_call(
        functools.partial(rotate_kernel, tiles),
        out_shape=jax.ShapeDtypeStruct((samples, both), F32),
        in_specs=[pl.BlockSpec(memory_space=pltpu.VMEM)] * 3,
        out_specs=pl.BlockSpec(memory_space=pltpu.HBM),
        scratch_shapes=[pltpu.VMEM((samples, both), F32), pltpu.SemaphoreType.DMA((len(tiles),))],
        compiler_params=pltpu.CompilerParams(vmem_limit_bytes=20 * 2**20),
        name="rotate",
    )(pair, high, low)


def solution(mesh):
    spec = P("row", "pair")
    return jax.shard_map(
        functools.partial(shards, mesh.shape["pair"]),
        mesh=mesh, in_specs=(spec,), out_specs=spec, check_vma=False,
    )
```

```python
import functools

import jax
import jax.numpy as jnp
from jax import lax
from jax.experimental import pallas as pl
from jax.experimental.pallas import tpu as pltpu
from jax.sharding import PartitionSpec as P

MESH = pl.DeviceIdType.MESH
F32 = jnp.float32
BF16 = jnp.bfloat16
EXTRA = 8
PIECES = 1


def split(value):
    high = value.astype(BF16)
    return high, (value - high.astype(F32)).astype(BF16)


def dot(left, right, dims):
    return lax.dot_general(left, right, (dims, ((), ())), preferred_element_type=F32)


def dot3(left, right, dims=((1,), (0,))):
    lh, ll = left
    rh, rl = right
    return dot(lh, rh, dims) + (dot(lh, rl, dims) + dot(ll, rh, dims))


def inner(left, right):
    return dot3(left, right, ((0,), (0,)))


def column_sums(value):
    rows, width = value.shape
    return jnp.sum((value * value).reshape(rows // EXTRA, EXTRA, width), axis=0)


def angles(cross, first, second):
    width = cross.shape[0]
    first = jnp.broadcast_to(first, (width, width)).T
    second = jnp.broadcast_to(second, (width, width))
    gap = second - first
    raw = cross * gap / (gap * gap + first * second + 1e-06)
    total = jnp.sum(jnp.sum(raw * raw, axis=0, keepdims=True), axis=1, keepdims=True)
    return raw, 1.0 / (1.0 + jnp.sqrt(total))


def polynomial(square, ident):
    halves = split(square)
    second = dot3(halves, halves)
    factor = 0.375 * ident - 0.3125 * square + 0.0625 * second
    return ident - 0.5 * square + dot3(split(second), split(factor))


def write_turn(theta, scale, high_ref, low_ref):
    width = theta.shape[0]
    rows = lax.broadcasted_iota(jnp.int32, (width, width), 0)
    cols = lax.broadcasted_iota(jnp.int32, (width, width), 1)
    ident = jnp.where(rows == cols, 1.0, 0.0).astype(F32)
    plain = split(theta)
    flipped = split(theta.T)
    upper = polynomial(dot3(plain, flipped) * (scale * scale), ident)
    lower = polynomial(dot3(flipped, plain) * (scale * scale), ident)
    off = dot3(split(upper), plain) * scale
    one, two = pl.ds(0, width), pl.ds(width, width)
    for half, at, block in ((0, one, upper), (1, one, off), (0, two, -off.T), (1, two, lower)):
        high, low = split(block)
        high_ref[half, at] = high
        low_ref[half, at] = low


def exchange_kernel(
    n_pair, chunk, load, early, extra,
    x_ref, pair_ref, high_ref, low_ref,
    x, out, raw, part, got, full, theta_own, thetas, turn_high, turn_low, early_high, early_low, relay,
    load_sem, send_sem, recv_sem, raw_send, raw_recv, theta_send, theta_recv, share_send, share_recv, row_send, row_recv,
    relay_send, relay_recv, far,
):
    p = lax.axis_index("pair")
    row = lax.axis_index("row")
    core = lax.rem(row, 2)
    mate = row + 1 - 2 * core
    across = lax.rem(row + 2, 4)
    others = (mate, across, 3 - row)
    samples, both = x.shape
    width = both // 2
    main = samples - early
    n_chunks = main // chunk
    n_direct = n_chunks - extra // chunk
    n_hops = (early + extra) // chunk
    first = p == 0
    last = p == n_pair - 1
    not_first = jnp.logical_not(first)
    not_last = jnp.logical_not(last)
    seam = n_pair // 2
    before = p == seam - 1
    after = p == seam
    ends = jnp.logical_or(first, last)
    middle = jnp.logical_or(before, after)
    rightward = jnp.logical_and(not_last, jnp.logical_not(before))
    leftward = jnp.logical_and(not_first, jnp.logical_not(after))
    inside = (jnp.logical_and(not_first, jnp.logical_not(after)), jnp.logical_and(not_last, jnp.logical_not(before)))
    halves = pl.ds(0, width), pl.ds(width, width)

    loads = []
    for i in range(samples // load):
        at = pl.ds(i * load, load)
        loads.append(pltpu.make_async_copy(x_ref.at[at], x.at[at], load_sem.at[i]))
        loads[-1].start()

    barrier = pltpu.get_barrier_semaphore()

    def greet(**where):
        pl.semaphore_signal(barrier, inc=1, device_id=where, device_id_type=MESH)

    for other in others:
        greet(row=other)

    def meet():
        @pl.when(jnp.logical_and(not_first, jnp.logical_not(after)))
        def _():
            greet(pair=p - 1)

        @pl.when(jnp.logical_and(not_last, jnp.logical_not(before)))
        def _():
            greet(pair=p + 1)

        @pl.when(first)
        def _():
            greet(pair=seam - 1)
            greet(pair=seam)

        @pl.when(last)
        def _():
            greet(pair=seam - 1)

        @pl.when(after)
        def _():
            greet(pair=seam - 1)
            greet(pair=n_pair - 1)

    meet()

    def met():
        @pl.when(first)
        def _():
            pl.semaphore_wait(barrier, 4)

        @pl.when(before)
        def _():
            pl.semaphore_wait(barrier, 7)
            for there in (0, seam):
                pl.semaphore_signal(far, inc=1, device_id={"pair": there}, device_id_type=MESH)

        @pl.when(jnp.logical_not(jnp.logical_or(first, before)))
        def _():
            pl.semaphore_wait(barrier, 5)

    def send(src, dst, send_sem, recv_sem, **where):
        return pltpu.make_async_remote_copy(
            src_ref=src, dst_ref=dst, send_sem=send_sem, recv_sem=recv_sem, device_id=where, device_id_type=MESH
        )

    def raw_copy(side, **where):
        return send(x_ref.at[pl.ds(main, early)], raw.at[side], raw_send.at[side], raw_recv.at[side], **where)

    def raw_start():
        @pl.when(rightward)
        def _():
            raw_copy(0, pair=p + 1).start()

        @pl.when(leftward)
        def _():
            raw_copy(1, pair=p - 1).start()

    size = width // 2
    step = size // PIECES

    def piece(k):
        return pl.ds(k * step, step + (EXTRA if k == PIECES - 1 else 0))

    def row_copies(turn, k):
        def along(src, dst, stage, other):
            return send(src, dst, row_send.at[turn, stage, k], row_recv.at[turn, stage, k], row=other)

        return (
            along(part.at[turn, 1 - core, piece(k)], got.at[turn, 0, piece(k)], 0, mate),
            along(part.at[turn, core, piece(k)], got.at[turn, 1, piece(k)], 1, across),
            along(full.at[turn, core, piece(k)], full.at[turn, core, piece(k)], 2, mate),
        )

    def add_half(turn, ref, at, h, fresh=False):
        left = ref[at, pl.ds(pl.multiple_of(h * size, size), size)]
        value = inner(split(left), split(ref[at, halves[1]]))
        if fresh:
            part[turn, h, pl.ds(0, size)] = value
        else:
            part[turn, h, pl.ds(0, size)] += value

    def add_sums(turn, ref, at, fresh=False):
        for h in range(2):
            value = column_sums(ref[at, halves[h]])
            if fresh:
                part[turn, h, pl.ds(size, EXTRA)] = value
            else:
                part[turn, h, pl.ds(size, EXTRA)] += value

    def add_gram(turn, ref, at):
        value = inner(split(ref[at, halves[0]]), split(ref[at, halves[1]]))
        for h in range(2):
            part[turn, h, pl.ds(0, size)] += value[h * size : (h + 1) * size]
        add_sums(turn, ref, at)

    def row_sum(turn, finish_own, meanwhile=lambda: None):
        copies = [row_copies(turn, k) for k in range(PIECES)]
        for one, _, _ in copies:
            one.start()
        finish_own()
        for k, (one, two, _) in enumerate(copies):
            one.wait_recv()
            part[turn, core, piece(k)] += got[turn, 0, piece(k)]
            two.start()
        meanwhile()
        for k, (_, two, three) in enumerate(copies):
            two.wait_recv()
            full[turn, core, piece(k)] = part[turn, core, piece(k)] + got[turn, 1, piece(k)]
            three.start()
        for _, _, three in copies:
            three.wait_recv()
        cross = jnp.concatenate([full[turn, 0, pl.ds(0, size)], full[turn, 1, pl.ds(0, size)]], axis=0)
        diag = [jnp.sum(full[turn, h, pl.ds(size, EXTRA)], axis=0, keepdims=True) for h in range(2)]
        return angles(cross, *diag)

    met()
    raw_start()
    for i in range(samples // load):
        loads[i].wait()
        at = pl.ds(i * load, load)
        add_sums(0, x, at, i == 0)
        add_half(0, x, at, 1 - core, i == 0)

    def finish_own():
        for i in range(2):
            add_half(0, x, pl.ds(i * (samples // 2), samples // 2), core, i == 0)

    raw_angles, scale = row_sum(0, finish_own)
    theta_own[...] = raw_angles * scale

    def quarter(of):
        return pl.ds(pl.multiple_of(of * (width // 4), width // 4), width // 4)

    def theta_copy(side, q, **where):
        at = quarter((row, across)[q])
        return send(theta_own.at[at], thetas.at[side, at], theta_send.at[side, q], theta_recv.at[side, q], **where)

    @pl.when(rightward)
    def _():
        theta_copy(0, 0, pair=p + 1).start()

    @pl.when(leftward)
    def _():
        theta_copy(1, 0, pair=p - 1).start()

    @pl.when(p == n_pair - 2)
    def _():
        theta_copy(0, 1, pair=p + 1).start()

    @pl.when(p == 1)
    def _():
        theta_copy(1, 1, pair=p - 1).start()

    write_turn(raw_angles, scale, turn_high, turn_low)

    def rows_of(i):
        return pl.ds(pl.multiple_of(i * chunk, chunk), chunk)

    def to(half, side, i, **where):
        return send(
            out.at[half, rows_of(i)], pair_ref.at[rows_of(i), halves[side]],
            send_sem.at[side, i], recv_sem.at[side, i], **where,
        )

    def keep(side, i):
        return pltpu.make_async_copy(out.at[0, rows_of(i)], pair_ref.at[rows_of(i), halves[side]], recv_sem.at[side, i])

    def goes_right(i):
        return jnp.logical_and(not_last, jnp.logical_or(jnp.logical_not(before), i < n_direct))

    def goes_left(i):
        return jnp.logical_and(not_first, jnp.logical_or(jnp.logical_not(after), i < n_direct))

    def rotate(i, carry):
        at = rows_of(i)
        value = split(x[at])
        top, bot = (dot3(value, (turn_high[h], turn_low[h])) for h in range(2))
        out[0, at] = top
        out[1, at] = bot

        @pl.when(first)
        def _():
            to(1, 0, i, pair=p + 1).start()
            keep(0, i).start()

        @pl.when(jnp.logical_and(not_first, goes_right(i)))
        def _():
            to(0, 0, i, pair=p + 1).start()

        @pl.when(goes_left(i))
        def _():
            to(1, 1, i, pair=p - 1).start()

        @pl.when(last)
        def _():
            keep(1, i).start()

        return carry

    end = pl.ds(main, early)

    def hop(stage, k, src, dst, **where):
        return send(src, dst, relay_send.at[stage, k], relay_recv.at[stage, k], **where)

    def hop_out(k, **where):
        at = pl.ds(k * chunk, chunk)
        return hop(0, k, relay.at[0, at], relay.at[1, at], **where)

    def hop_on(side, k, **where):
        to_rows = pl.ds(samples - early - extra + k * chunk, chunk)
        return hop(1, k, relay.at[1, pl.ds(k * chunk, chunk)], pair_ref.at[to_rows, halves[side]], **where)

    @pl.when(after)
    def _():
        pl.semaphore_wait(far, 1)

    for half, here, there in ((0, before, n_pair - 1), (1, after, 0)):

        @pl.when(here)
        def _(half=half, there=there):
            for k in range(n_hops):
                value = split(x[pl.ds(samples - early - extra + k * chunk, chunk)])
                relay[0, pl.ds(k * chunk, chunk)] = dot3(value, (turn_high[half], turn_low[half]))
                hop_out(k, pair=there).start()

    lax.fori_loop(0, n_chunks, rotate, 0)

    for side, here, there in ((0, last, seam), (1, first, seam - 1)):

        @pl.when(here)
        def _(side=side, there=there):
            if side == 1:
                pl.semaphore_wait(far, 1)
            for k in range(n_hops):
                hop_out(k, pair=there).wait_recv()
                hop_on(side, k, pair=there).start()

    def share(side, k, q, of):
        at = quarter(of)
        return send(thetas.at[side, at], thetas.at[side, at], share_send.at[side, k + q], share_recv.at[side, k + q], row=others[k])

    edge = (first, last)
    wide = (last, first)
    narrow = tuple(jnp.logical_and(inside[side], jnp.logical_not(wide[side])) for side in range(2))
    for side in range(2):

        @pl.when(narrow[side])
        def _(side=side):
            theta_copy(side, 0, pair=p).wait_recv()
            for k in range(3):
                share(side, k, 0, row).start()

        @pl.when(wide[side])
        def _(side=side):
            for q in range(2):
                theta_copy(side, q, pair=p).wait_recv()
                share(side, 0, q, (row, across)[q]).start()

        @pl.when(edge[side])
        def _(side=side):
            thetas[side] = theta_own[...]
            raw[side] = x[end]

    for side in range(2):

        @pl.when(narrow[side])
        def _(side=side):
            for k in range(3):
                share(side, k, 0, others[k]).wait_recv()

        @pl.when(wide[side])
        def _(side=side):
            for q in range(2):
                share(side, 0, q, (mate, 3 - row)[q]).wait_recv()

        @pl.when(inside[side])
        def _(side=side):
            raw_copy(side, pair=p).wait_recv()

        @pl.when(jnp.logical_not((after, before)[side]))
        def _(side=side):
            write_turn(thetas[side], 1.0, early_high, early_low)
            half = (p == 1).astype(jnp.int32) if side == 0 else not_last.astype(jnp.int32)
            pair_ref[end, halves[side]] = dot3(split(raw[side]), (early_high[half], early_low[half]))

    part[1] = jnp.zeros_like(part[1])

    def arrive(i):
        @pl.when(jnp.logical_or(jnp.logical_not(after), i < n_direct))
        def _():
            keep(0, i).wait()

        @pl.when(jnp.logical_or(jnp.logical_not(before), i < n_direct))
        def _():
            keep(1, i).wait()

        @pl.when(i == n_direct)
        def _():
            for side in range(2):

                @pl.when((after, before)[side])
                def _(side=side):
                    for k in range(n_hops):
                        hop_on(side, k, pair=p).wait_recv()

            add_gram(1, pair_ref, end)


    def receive(i, carry):
        arrive(i)
        add_gram(1, pair_ref, rows_of(i))
        return carry

    lax.fori_loop(0, n_chunks - 1, receive, 0)
    arrive(n_chunks - 1)
    tail = pl.ds((n_chunks - 1) * chunk, chunk)
    add_sums(1, pair_ref, tail)
    add_half(1, pair_ref, tail, 1 - core)
    def drain():
        def finish(i, carry):
            @pl.when(goes_right(i))
            def _():
                to(0, 0, i, pair=p + 1).wait_send()

            @pl.when(goes_left(i))
            def _():
                to(1, 1, i, pair=p - 1).wait_send()

            return carry

        lax.fori_loop(0, n_chunks, finish, 0)
        for k in range(PIECES):
            for copy in row_copies(0, k):
                copy.wait_send()
        for side, goes, twice in ((0, rightward, p == n_pair - 2), (1, leftward, p == 1)):

            @pl.when(goes)
            def _(side=side):
                theta_copy(side, 0, pair=p).wait_send()
                raw_copy(side, pair=p).wait_send()

            @pl.when(twice)
            def _(side=side):
                theta_copy(side, 1, pair=p).wait_send()

            @pl.when(narrow[side])
            def _(side=side):
                for k in range(3):
                    share(side, k, 0, row).wait_send()

            @pl.when(wide[side])
            def _(side=side):
                for q in range(2):
                    share(side, 0, q, (row, across)[q]).wait_send()
                for k in range(n_hops):
                    hop_on(side, k, pair=p).wait_send()

        @pl.when(middle)
        def _():
            for k in range(n_hops):
                hop_out(k, pair=p).wait_send()

    write_turn(*row_sum(1, lambda: add_half(1, pair_ref, tail, core), drain), high_ref, low_ref)
    for k in range(PIECES):
        for copy in row_copies(1, k):
            copy.wait_send()


def rotate_kernel(tiles, x_ref, high_ref, low_ref, out_ref, out, sem):
    copies = []
    at = 0
    for k, rows in enumerate(tiles):
        part = pl.ds(at, rows)
        value = split(x_ref[part])
        out[part] = jnp.concatenate([dot3(value, (high_ref[h], low_ref[h])) for h in range(2)], axis=1)
        copies.append(pltpu.make_async_copy(out.at[part], out_ref.at[part], sem.at[k]))
        copies[-1].start()
        at += rows
    for copy in copies:
        copy.wait()


def shards(n_pair, states):
    samples, both = states.shape
    width = both // 2
    chunk = 128
    load = 512
    early = 256
    extra = 512
    main = samples - early
    n_chunks = main // chunk
    turn = (2, both, width)
    pair, high, low = pl.pallas_call(
        functools.partial(exchange_kernel, n_pair, chunk, load, early, extra),
        out_shape=[pltpu.VMEM((samples, both), F32), pltpu.VMEM(turn, BF16), pltpu.VMEM(turn, BF16)],
        in_specs=[pl.BlockSpec(memory_space=pltpu.HBM)],
        out_specs=[pl.BlockSpec(memory_space=pltpu.VMEM)] * 3,
        scratch_shapes=[
            pltpu.VMEM((samples, both), F32),
            pltpu.VMEM((2, main, width), F32),
            pltpu.VMEM((2, early, both), F32),
            pltpu.VMEM((2, 2, width // 2 + EXTRA, width), F32),
            pltpu.VMEM((2, 2, width // 2 + EXTRA, width), F32),
            pltpu.VMEM((2, 2, width // 2 + EXTRA, width), F32),
            pltpu.VMEM((width, width), F32),
            pltpu.VMEM((2, width, width), F32),
            pltpu.VMEM(turn, BF16),
            pltpu.VMEM(turn, BF16),
            pltpu.VMEM(turn, BF16),
            pltpu.VMEM(turn, BF16),
            pltpu.VMEM((2, early + extra, width), F32),
            pltpu.SemaphoreType.DMA((samples // load,)),
            pltpu.SemaphoreType.DMA((2, n_chunks)),
            pltpu.SemaphoreType.DMA((2, n_chunks)),
            pltpu.SemaphoreType.DMA((2,)),
            pltpu.SemaphoreType.DMA((2,)),
            pltpu.SemaphoreType.DMA((2, 2)),
            pltpu.SemaphoreType.DMA((2, 2)),
            pltpu.SemaphoreType.DMA((2, 3)),
            pltpu.SemaphoreType.DMA((2, 3)),
            pltpu.SemaphoreType.DMA((2, 3, PIECES)),
            pltpu.SemaphoreType.DMA((2, 3, PIECES)),
            pltpu.SemaphoreType.DMA((2, (early + extra) // chunk)),
            pltpu.SemaphoreType.DMA((2, (early + extra) // chunk)),
            pltpu.SemaphoreType.REGULAR,
        ],
        compiler_params=pltpu.CompilerParams(
            collective_id=0, has_side_effects=True, vmem_limit_bytes=40 * 2**20
        ),
        name="exchange",
    )(pltpu.with_memory_space_constraint(states, pltpu.HBM))
    tiles = (512, 512, 512, 256, 256)
    return pl.pallas_call(
        functools.partial(rotate_kernel, tiles),
        out_shape=jax.ShapeDtypeStruct((samples, both), F32),
        in_specs=[pl.BlockSpec(memory_space=pltpu.VMEM)] * 3,
        out_specs=pl.BlockSpec(memory_space=pltpu.HBM),
        scratch_shapes=[pltpu.VMEM((samples, both), F32), pltpu.SemaphoreType.DMA((len(tiles),))],
        compiler_params=pltpu.CompilerParams(vmem_limit_bytes=20 * 2**20),
        name="rotate",
    )(pair, high, low)


def solution(mesh):
    spec = P("row", "pair")
    return jax.shard_map(
        functools.partial(shards, mesh.shape["pair"]),
        mesh=mesh, in_specs=(spec,), out_specs=spec, check_vma=False,
    )
```

```python
import functools

import jax
import jax.numpy as jnp
from jax import lax
from jax.experimental import pallas as pl
from jax.experimental.pallas import tpu as pltpu
from jax.sharding import PartitionSpec as P

MESH = pl.DeviceIdType.MESH
F32 = jnp.float32
BF16 = jnp.bfloat16
EXTRA = 8
PIECES = 1


def split(value):
    high = value.astype(BF16)
    return high, (value - high.astype(F32)).astype(BF16)


def dot(left, right, dims):
    return lax.dot_general(left, right, (dims, ((), ())), preferred_element_type=F32)


def dot3(left, right, dims=((1,), (0,))):
    lh, ll = left
    rh, rl = right
    return dot(lh, rh, dims) + (dot(lh, rl, dims) + dot(ll, rh, dims))


def inner(left, right):
    return dot3(left, right, ((0,), (0,)))


def column_sums(value):
    rows, width = value.shape
    return jnp.sum((value * value).reshape(rows // EXTRA, EXTRA, width), axis=0)


def angles(cross, first, second):
    width = cross.shape[0]
    first = jnp.broadcast_to(first, (width, width)).T
    second = jnp.broadcast_to(second, (width, width))
    gap = second - first
    raw = cross * gap / (gap * gap + first * second + 1e-06)
    total = jnp.sum(jnp.sum(raw * raw, axis=0, keepdims=True), axis=1, keepdims=True)
    return raw, 1.0 / (1.0 + jnp.sqrt(total))


def polynomial(square, ident):
    halves = split(square)
    second = dot3(halves, halves)
    factor = 0.375 * ident - 0.3125 * square + 0.0625 * second
    return ident - 0.5 * square + dot3(split(second), split(factor))


def write_turn(theta, scale, high_ref, low_ref):
    width = theta.shape[0]
    rows = lax.broadcasted_iota(jnp.int32, (width, width), 0)
    cols = lax.broadcasted_iota(jnp.int32, (width, width), 1)
    ident = jnp.where(rows == cols, 1.0, 0.0).astype(F32)
    plain = split(theta)
    flipped = split(theta.T)
    upper = polynomial(dot3(plain, flipped) * (scale * scale), ident)
    lower = polynomial(dot3(flipped, plain) * (scale * scale), ident)
    off = dot3(split(upper), plain) * scale
    one, two = pl.ds(0, width), pl.ds(width, width)
    for half, at, block in ((0, one, upper), (1, one, off), (0, two, -off.T), (1, two, lower)):
        high, low = split(block)
        high_ref[half, at] = high
        low_ref[half, at] = low


def exchange_kernel(
    n_pair, chunk, load, early, extra,
    x_ref, pair_ref, high_ref, low_ref,
    x, out, raw, part, got, full, theta_own, thetas, turn_high, turn_low, early_high, early_low, relay,
    load_sem, send_sem, recv_sem, raw_send, raw_recv, theta_send, theta_recv, share_send, share_recv, row_send, row_recv,
    relay_send, relay_recv, far,
):
    p = lax.axis_index("pair")
    row = lax.axis_index("row")
    core = lax.rem(row, 2)
    mate = row + 1 - 2 * core
    across = lax.rem(row + 2, 4)
    others = (mate, across, 3 - row)
    samples, both = x.shape
    width = both // 2
    main = samples - early
    n_chunks = main // chunk
    n_direct = n_chunks - extra // chunk
    n_hops = (early + extra) // chunk
    first = p == 0
    last = p == n_pair - 1
    not_first = jnp.logical_not(first)
    not_last = jnp.logical_not(last)
    seam = n_pair // 2
    before = p == seam - 1
    after = p == seam
    ends = jnp.logical_or(first, last)
    middle = jnp.logical_or(before, after)
    rightward = jnp.logical_and(not_last, jnp.logical_not(before))
    leftward = jnp.logical_and(not_first, jnp.logical_not(after))
    inside = (jnp.logical_and(not_first, jnp.logical_not(after)), jnp.logical_and(not_last, jnp.logical_not(before)))
    halves = pl.ds(0, width), pl.ds(width, width)

    loads = []
    for i in range(samples // load):
        at = pl.ds(i * load, load)
        loads.append(pltpu.make_async_copy(x_ref.at[at], x.at[at], load_sem.at[i]))
        loads[-1].start()

    barrier = pltpu.get_barrier_semaphore()

    def greet(**where):
        pl.semaphore_signal(barrier, inc=1, device_id=where, device_id_type=MESH)

    for other in others:
        greet(row=other)

    def meet():
        @pl.when(jnp.logical_and(not_first, jnp.logical_not(after)))
        def _():
            greet(pair=p - 1)

        @pl.when(jnp.logical_and(not_last, jnp.logical_not(before)))
        def _():
            greet(pair=p + 1)

        @pl.when(first)
        def _():
            greet(pair=seam - 1)
            greet(pair=seam)

        @pl.when(last)
        def _():
            greet(pair=seam - 1)

        @pl.when(after)
        def _():
            greet(pair=seam - 1)
            greet(pair=n_pair - 1)

    meet()

    def met():
        @pl.when(first)
        def _():
            pl.semaphore_wait(barrier, 4)

        @pl.when(before)
        def _():
            pl.semaphore_wait(barrier, 7)
            for there in (0, seam):
                pl.semaphore_signal(far, inc=1, device_id={"pair": there}, device_id_type=MESH)

        @pl.when(jnp.logical_not(jnp.logical_or(first, before)))
        def _():
            pl.semaphore_wait(barrier, 5)

    def send(src, dst, send_sem, recv_sem, **where):
        return pltpu.make_async_remote_copy(
            src_ref=src, dst_ref=dst, send_sem=send_sem, recv_sem=recv_sem, device_id=where, device_id_type=MESH
        )

    def raw_copy(side, **where):
        return send(x_ref.at[pl.ds(main, early)], raw.at[side], raw_send.at[side], raw_recv.at[side], **where)

    def raw_start():
        @pl.when(rightward)
        def _():
            raw_copy(0, pair=p + 1).start()

        @pl.when(leftward)
        def _():
            raw_copy(1, pair=p - 1).start()

    size = width // 2
    step = size // PIECES

    def piece(k):
        return pl.ds(k * step, step + (EXTRA if k == PIECES - 1 else 0))

    def row_copies(turn, k):
        def along(src, dst, stage, other):
            return send(src, dst, row_send.at[turn, stage, k], row_recv.at[turn, stage, k], row=other)

        return (
            along(part.at[turn, 1 - core, piece(k)], got.at[turn, 0, piece(k)], 0, mate),
            along(part.at[turn, core, piece(k)], got.at[turn, 1, piece(k)], 1, across),
            along(full.at[turn, core, piece(k)], full.at[turn, core, piece(k)], 2, mate),
        )

    def add_half(turn, ref, at, h, fresh=False):
        left = ref[at, pl.ds(pl.multiple_of(h * size, size), size)]
        value = inner(split(left), split(ref[at, halves[1]]))
        if fresh:
            part[turn, h, pl.ds(0, size)] = value
        else:
            part[turn, h, pl.ds(0, size)] += value

    def add_sums(turn, ref, at, fresh=False):
        for h in range(2):
            value = column_sums(ref[at, halves[h]])
            if fresh:
                part[turn, h, pl.ds(size, EXTRA)] = value
            else:
                part[turn, h, pl.ds(size, EXTRA)] += value

    def add_gram(turn, ref, at):
        value = inner(split(ref[at, halves[0]]), split(ref[at, halves[1]]))
        for h in range(2):
            part[turn, h, pl.ds(0, size)] += value[h * size : (h + 1) * size]
        add_sums(turn, ref, at)

    def row_sum(turn, finish_own, meanwhile=lambda: None):
        copies = [row_copies(turn, k) for k in range(PIECES)]
        for one, _, _ in copies:
            one.start()
        finish_own()
        for k, (one, two, _) in enumerate(copies):
            one.wait_recv()
            part[turn, core, piece(k)] += got[turn, 0, piece(k)]
            two.start()
        meanwhile()
        for k, (_, two, three) in enumerate(copies):
            two.wait_recv()
            full[turn, core, piece(k)] = part[turn, core, piece(k)] + got[turn, 1, piece(k)]
            three.start()
        for _, _, three in copies:
            three.wait_recv()
        cross = jnp.concatenate([full[turn, 0, pl.ds(0, size)], full[turn, 1, pl.ds(0, size)]], axis=0)
        diag = [jnp.sum(full[turn, h, pl.ds(size, EXTRA)], axis=0, keepdims=True) for h in range(2)]
        return angles(cross, *diag)

    met()
    raw_start()
    for i in range(samples // load):
        loads[i].wait()
        at = pl.ds(i * load, load)
        add_sums(0, x, at, i == 0)
        add_half(0, x, at, 1 - core, i == 0)

    def finish_own():
        for i in range(2):
            add_half(0, x, pl.ds(i * (samples // 2), samples // 2), core, i == 0)

    raw_angles, scale = row_sum(0, finish_own)
    theta_own[...] = raw_angles * scale

    def quarter(of):
        return pl.ds(pl.multiple_of(of * (width // 4), width // 4), width // 4)

    def theta_copy(side, q, **where):
        at = quarter((row, across)[q])
        return send(theta_own.at[at], thetas.at[side, at], theta_send.at[side, q], theta_recv.at[side, q], **where)

    @pl.when(rightward)
    def _():
        theta_copy(0, 0, pair=p + 1).start()

    @pl.when(leftward)
    def _():
        theta_copy(1, 0, pair=p - 1).start()

    @pl.when(p == n_pair - 2)
    def _():
        theta_copy(0, 1, pair=p + 1).start()

    @pl.when(p == 1)
    def _():
        theta_copy(1, 1, pair=p - 1).start()

    write_turn(raw_angles, scale, turn_high, turn_low)

    def rows_of(i):
        return pl.ds(pl.multiple_of(i * chunk, chunk), chunk)

    def to(half, side, i, **where):
        return send(
            out.at[half, rows_of(i)], pair_ref.at[rows_of(i), halves[side]],
            send_sem.at[side, i], recv_sem.at[side, i], **where,
        )

    def keep(side, i):
        return pltpu.make_async_copy(out.at[0, rows_of(i)], pair_ref.at[rows_of(i), halves[side]], recv_sem.at[side, i])

    def goes_right(i):
        return jnp.logical_and(not_last, jnp.logical_or(jnp.logical_not(before), i < n_direct))

    def goes_left(i):
        return jnp.logical_and(not_first, jnp.logical_or(jnp.logical_not(after), i < n_direct))

    def rotate(i, carry):
        at = rows_of(i)
        value = split(x[at])
        top, bot = (dot3(value, (turn_high[h], turn_low[h])) for h in range(2))
        out[0, at] = top
        out[1, at] = bot

        @pl.when(first)
        def _():
            to(1, 0, i, pair=p + 1).start()
            keep(0, i).start()

        @pl.when(jnp.logical_and(not_first, goes_right(i)))
        def _():
            to(0, 0, i, pair=p + 1).start()

        @pl.when(goes_left(i))
        def _():
            to(1, 1, i, pair=p - 1).start()

        @pl.when(last)
        def _():
            keep(1, i).start()

        return carry

    end = pl.ds(main, early)

    def hop(stage, k, src, dst, **where):
        return send(src, dst, relay_send.at[stage, k], relay_recv.at[stage, k], **where)

    def hop_out(k, **where):
        at = pl.ds(k * chunk, chunk)
        return hop(0, k, relay.at[0, at], relay.at[1, at], **where)

    def hop_on(side, k, **where):
        to_rows = pl.ds(samples - early - extra + k * chunk, chunk)
        return hop(1, k, relay.at[1, pl.ds(k * chunk, chunk)], pair_ref.at[to_rows, halves[side]], **where)

    @pl.when(after)
    def _():
        pl.semaphore_wait(far, 1)

    for half, here, there in ((0, before, n_pair - 1), (1, after, 0)):

        @pl.when(here)
        def _(half=half, there=there):
            for k in range(n_hops):
                value = split(x[pl.ds(samples - early - extra + k * chunk, chunk)])
                relay[0, pl.ds(k * chunk, chunk)] = dot3(value, (turn_high[half], turn_low[half]))
                hop_out(k, pair=there).start()

    lax.fori_loop(0, n_chunks, rotate, 0)

    for side, here, there in ((0, last, seam), (1, first, seam - 1)):

        @pl.when(here)
        def _(side=side, there=there):
            if side == 1:
                pl.semaphore_wait(far, 1)
            for k in range(n_hops):
                hop_out(k, pair=there).wait_recv()
                hop_on(side, k, pair=there).start()

    def share(side, k, q, of):
        at = quarter(of)
        return send(thetas.at[side, at], thetas.at[side, at], share_send.at[side, k + q], share_recv.at[side, k + q], row=others[k])

    edge = (first, last)
    wide = (last, first)
    narrow = tuple(jnp.logical_and(inside[side], jnp.logical_not(wide[side])) for side in range(2))
    for side in range(2):

        @pl.when(narrow[side])
        def _(side=side):
            theta_copy(side, 0, pair=p).wait_recv()
            for k in range(3):
                share(side, k, 0, row).start()

        @pl.when(wide[side])
        def _(side=side):
            for q in range(2):
                theta_copy(side, q, pair=p).wait_recv()
                share(side, 0, q, (row, across)[q]).start()

        @pl.when(edge[side])
        def _(side=side):
            thetas[side] = theta_own[...]
            raw[side] = x[end]

    for side in range(2):

        @pl.when(narrow[side])
        def _(side=side):
            for k in range(3):
                share(side, k, 0, others[k]).wait_recv()

        @pl.when(wide[side])
        def _(side=side):
            for q in range(2):
                share(side, 0, q, (mate, 3 - row)[q]).wait_recv()

        @pl.when(inside[side])
        def _(side=side):
            raw_copy(side, pair=p).wait_recv()

        @pl.when(jnp.logical_not((after, before)[side]))
        def _(side=side):
            write_turn(thetas[side], 1.0, early_high, early_low)
            half = (p == 1).astype(jnp.int32) if side == 0 else not_last.astype(jnp.int32)
            pair_ref[end, halves[side]] = dot3(split(raw[side]), (early_high[half], early_low[half]))

    part[1] = jnp.zeros_like(part[1])

    def arrive(i):
        @pl.when(jnp.logical_or(jnp.logical_not(after), i < n_direct))
        def _():
            keep(0, i).wait()

        @pl.when(jnp.logical_or(jnp.logical_not(before), i < n_direct))
        def _():
            keep(1, i).wait()

        @pl.when(i == n_direct)
        def _():
            for side in range(2):

                @pl.when((after, before)[side])
                def _(side=side):
                    for k in range(n_hops):
                        hop_on(side, k, pair=p).wait_recv()

            add_gram(1, pair_ref, end)


    def receive(i, carry):
        arrive(i)
        add_gram(1, pair_ref, rows_of(i))
        return carry

    lax.fori_loop(0, n_chunks - 1, receive, 0)
    arrive(n_chunks - 1)
    tail = pl.ds((n_chunks - 1) * chunk, chunk)
    add_sums(1, pair_ref, tail)
    add_half(1, pair_ref, tail, 1 - core)
    def drain():
        def finish(i, carry):
            @pl.when(goes_right(i))
            def _():
                to(0, 0, i, pair=p + 1).wait_send()

            @pl.when(goes_left(i))
            def _():
                to(1, 1, i, pair=p - 1).wait_send()

            return carry

        lax.fori_loop(0, n_chunks, finish, 0)
        for k in range(PIECES):
            for copy in row_copies(0, k):
                copy.wait_send()
        for side, goes, twice in ((0, rightward, p == n_pair - 2), (1, leftward, p == 1)):

            @pl.when(goes)
            def _(side=side):
                theta_copy(side, 0, pair=p).wait_send()
                raw_copy(side, pair=p).wait_send()

            @pl.when(twice)
            def _(side=side):
                theta_copy(side, 1, pair=p).wait_send()

            @pl.when(narrow[side])
            def _(side=side):
                for k in range(3):
                    share(side, k, 0, row).wait_send()

            @pl.when(wide[side])
            def _(side=side):
                for q in range(2):
                    share(side, 0, q, (row, across)[q]).wait_send()
                for k in range(n_hops):
                    hop_on(side, k, pair=p).wait_send()

        @pl.when(middle)
        def _():
            for k in range(n_hops):
                hop_out(k, pair=p).wait_send()

    write_turn(*row_sum(1, lambda: add_half(1, pair_ref, tail, core), drain), high_ref, low_ref)
    for k in range(PIECES):
        for copy in row_copies(1, k):
            copy.wait_send()


def rotate_kernel(tiles, x_ref, high_ref, low_ref, out_ref, out, sem):
    copies = []
    at = 0
    for k, rows in enumerate(tiles):
        part = pl.ds(at, rows)
        value = split(x_ref[part])
        out[part] = jnp.concatenate([dot3(value, (high_ref[h], low_ref[h])) for h in range(2)], axis=1)
        copies.append(pltpu.make_async_copy(out.at[part], out_ref.at[part], sem.at[k]))
        copies[-1].start()
        at += rows
    for copy in copies:
        copy.wait()


def shards(n_pair, states):
    samples, both = states.shape
    width = both // 2
    chunk = 256
    load = 512
    early = 256
    extra = 512
    main = samples - early
    n_chunks = main // chunk
    turn = (2, both, width)
    pair, high, low = pl.pallas_call(
        functools.partial(exchange_kernel, n_pair, chunk, load, early, extra),
        out_shape=[pltpu.VMEM((samples, both), F32), pltpu.VMEM(turn, BF16), pltpu.VMEM(turn, BF16)],
        in_specs=[pl.BlockSpec(memory_space=pltpu.HBM)],
        out_specs=[pl.BlockSpec(memory_space=pltpu.VMEM)] * 3,
        scratch_shapes=[
            pltpu.VMEM((samples, both), F32),
            pltpu.VMEM((2, main, width), F32),
            pltpu.VMEM((2, early, both), F32),
            pltpu.VMEM((2, 2, width // 2 + EXTRA, width), F32),
            pltpu.VMEM((2, 2, width // 2 + EXTRA, width), F32),
            pltpu.VMEM((2, 2, width // 2 + EXTRA, width), F32),
            pltpu.VMEM((width, width), F32),
            pltpu.VMEM((2, width, width), F32),
            pltpu.VMEM(turn, BF16),
            pltpu.VMEM(turn, BF16),
            pltpu.VMEM(turn, BF16),
            pltpu.VMEM(turn, BF16),
            pltpu.VMEM((2, early + extra, width), F32),
            pltpu.SemaphoreType.DMA((samples // load,)),
            pltpu.SemaphoreType.DMA((2, n_chunks)),
            pltpu.SemaphoreType.DMA((2, n_chunks)),
            pltpu.SemaphoreType.DMA((2,)),
            pltpu.SemaphoreType.DMA((2,)),
            pltpu.SemaphoreType.DMA((2, 2)),
            pltpu.SemaphoreType.DMA((2, 2)),
            pltpu.SemaphoreType.DMA((2, 3)),
            pltpu.SemaphoreType.DMA((2, 3)),
            pltpu.SemaphoreType.DMA((2, 3, PIECES)),
            pltpu.SemaphoreType.DMA((2, 3, PIECES)),
            pltpu.SemaphoreType.DMA((2, (early + extra) // chunk)),
            pltpu.SemaphoreType.DMA((2, (early + extra) // chunk)),
            pltpu.SemaphoreType.REGULAR,
        ],
        compiler_params=pltpu.CompilerParams(
            collective_id=0, has_side_effects=True, vmem_limit_bytes=40 * 2**20
        ),
        name="exchange",
    )(pltpu.with_memory_space_constraint(states, pltpu.HBM))
    tiles = (512, 512, 512, 256, 256)
    return pl.pallas_call(
        functools.partial(rotate_kernel, tiles),
        out_shape=jax.ShapeDtypeStruct((samples, both), F32),
        in_specs=[pl.BlockSpec(memory_space=pltpu.VMEM)] * 3,
        out_specs=pl.BlockSpec(memory_space=pltpu.HBM),
        scratch_shapes=[pltpu.VMEM((samples, both), F32), pltpu.SemaphoreType.DMA((len(tiles),))],
        compiler_params=pltpu.CompilerParams(vmem_limit_bytes=20 * 2**20),
        name="rotate",
    )(pair, high, low)


def solution(mesh):
    spec = P("row", "pair")
    return jax.shard_map(
        functools.partial(shards, mesh.shape["pair"]),
        mesh=mesh, in_specs=(spec,), out_specs=spec, check_vma=False,
    )
```
